512 devices in a mesh: dp: 64 (over z, x), tensor: 8 (over y, core).
Axes of the slice: x: 4, y: 4, z: 16, core: 2. Of those that a mesh axis runs over, the one named last changes fastest.
Arguments:
- inputs_x: bfloat16 [16384, 8192], P('dp', 'tensor'), may hold values from -7 to 7
- gate_z: bfloat16 [16384, 8192], P('dp', 'tensor'), may hold values from -6 to 6
- input_b: bfloat16 [16384, 1024], P('dp', 'tensor'), may hold values from -1 to 1
- input_c: bfloat16 [16384, 1024], P('dp', 'tensor'), may hold values from -1 to 1
- dt_raw: float32 [16384, 128], P('dp', 'tensor'), may hold values from -3 to 3
- a_log: float32 [128], P('tensor'), may hold values from -8.5 to -2
- dt_bias: float32 [128], P('tensor'), may hold values from -3 to -1
- skip_d: float32 [128], P('tensor'), may hold values from 0.5 to 1.5
- norm_gain: float32 [8192], P('tensor'), may hold values from 0.1 to 1.9
- lengths: int32 [16], replicated, may hold values from 1 to 8192, 16256 in all
- cotangent: bfloat16 [16384, 8192], P('dp', 'tensor'), may hold values from -6 to 6
Outputs:
- grad_x: bfloat16 [16384, 8192], P('dp', 'tensor')
- grad_b: bfloat16 [16384, 1024], P('dp', 'tensor')
- grad_c: bfloat16 [16384, 1024], P('dp', 'tensor')
- grad_dt: float32 [16384, 128], P('dp', 'tensor')
- grad_gain: float32 [8192], P(('tensor', 'dp'))
The draws below stay inside these ranges and needn't reach their ends.
Inputs may be any that keep to these rules, and one draw needn't show every extreme that they name: `lengths`: each document holds 1 to 8192 tokens and one holds exactly 8192; together they fill exactly the first 16256 positions, and the last 128 positions are padding.
All inputs are finite; a program needn't handle non-finite values.
Results may differ from the reference program's by a relative error of at most 0.0011.
Values sent between devices are 32-bit elements; how exact they have to be, the bound alone decides.
No kernel may reach another device: no remote copies, remote signals or barrier semaphores. Data moves between devices by JAX's collectives and lax.ppermute only.
A program may use at most 128 MiB of HBM per device.

```python
import math
import jax
import jax.numpy as jnp
import numpy as np
from jax import lax

HEADS = 128
HEAD_DIM = 64
STATE = 128
GROUPS = 8
STRETCH = 128
DOCS = 16
SEQ = 16384
DOC_MOST = 8192
INNER = 8192


def head_rates(key, lowest, spread):
    return lowest + spread * jax.random.uniform(jax.random.fold_in(key, 101), (HEADS,), jnp.float32)


def state_signs(key):
    flip_bits = jax.random.bernoulli(jax.random.fold_in(key, 202), 0.5, (GROUPS * STATE,))
    return jnp.where(flip_bits, 1.0, -1.0).astype(jnp.float32)


def draw_a_log(key, part):
    head_values = head_rates(key, -8.5, 6.5)
    return head_values.astype(jnp.float32)


def draw_inputs_x(key, part):
    head_values = head_rates(key, -8.5, 6.5)
    key = jax.random.fold_in(key, 2)
    sign_key, span_key, noise_key = jax.random.split(key, 3)
    magnitude = jnp.minimum(jnp.exp(head_values + 3.5), 1.0)
    channel_signs = jnp.where(jax.random.bernoulli(sign_key, 0.5, (HEADS, HEAD_DIM)), 1.0, -1.0)
    active_spans = jnp.where(jax.random.bernoulli(span_key, 0.3, (SEQ // STRETCH,)), 1.0, 0.0)
    span_rows = jnp.repeat(active_spans, STRETCH, total_repeat_length=SEQ)
    common_part = span_rows[:, None] * (magnitude[:, None] * channel_signs).reshape(1, HEADS * HEAD_DIM)
    noise_part = jax.random.normal(noise_key, (SEQ, HEADS * HEAD_DIM), jnp.float32)
    return jnp.clip(noise_part + common_part, -7.0, 7.0).astype(jnp.bfloat16)


def draw_input_b(key, part):
    entry_signs = state_signs(key)
    key = jax.random.fold_in(key, 3)
    size_key, noise_key = jax.random.split(key)
    entry_sizes = jax.random.uniform(size_key, (GROUPS * STATE,), jnp.float32, 0.04, 0.1)
    noise_part = 0.12 * jax.random.normal(noise_key, (SEQ, GROUPS * STATE), jnp.float32)
    return jnp.clip(noise_part + (entry_signs * entry_sizes)[None, :], -1.0, 1.0).astype(jnp.bfloat16)


def draw_input_c(key, part):
    entry_signs = state_signs(key)
    key = jax.random.fold_in(key, 4)
    size_key, noise_key = jax.random.split(key)
    entry_sizes = jax.random.uniform(size_key, (GROUPS * STATE,), jnp.float32, 0.04, 0.1)
    noise_part = 0.12 * jax.random.normal(noise_key, (SEQ, GROUPS * STATE), jnp.float32)
    return jnp.clip(noise_part + (entry_signs * entry_sizes)[None, :], -1.0, 1.0).astype(jnp.bfloat16)


def draw_dt_raw(key, part):
    key = jax.random.fold_in(key, 5)
    step_values = 0.5 * jax.random.normal(key, (SEQ, HEADS), jnp.float32) - 0.75
    return jnp.clip(step_values, -3.0, 3.0).astype(jnp.float32)


def levels(rng, extent, cuts, low, high):
    def one(dim, blocks):
        steps = jax.random.uniform(jax.random.fold_in(jax.random.fold_in(rng, 6), dim), (blocks,), jnp.float32, low / len(cuts), high / len(cuts))
        return jnp.repeat(jnp.exp(steps), extent[dim] // blocks).reshape((-1,) + (1,) * (len(extent) - dim - 1))

    loudness = one(*cuts[0])
    for cut in cuts[1:]:
        loudness = loudness * one(*cut)
    return loudness


def length_profile(number_of, total, most, lean):
    weights = [(1 << 20) // math.isqrt(rank ** lean) + 1 for rank in range(2, number_of + 1)]
    rest, given = total - most - (number_of - 1), [1] * (number_of - 1)
    while rest > 0:
        movable = [i for i in range(number_of - 1) if given[i] < most]
        mass, remaining = sum([weights[i] for i in movable]), rest
        for i in movable:
            addition = min(most - given[i], max(1, remaining * weights[i] // mass), rest)
            given[i] = given[i] + addition
            rest = rest - addition
    return np.array([most] + given)


def ragged(rng, amount, total, most, slope):
    if amount == 2:
        one = jax.random.randint(rng, (), max(1, total - most), min(most, total - 1) + 1)
        return jnp.stack([one, total - one])
    sizes = jnp.asarray(length_profile(amount, total, most, slope), jnp.int32)
    twos = (amount - 1) // 2
    source_of, sink = sizes[1:1 + 2 * twos:2], sizes[2:2 + 2 * twos:2]
    slack = jnp.minimum(source_of - 1, most - sink)
    moved = jax.random.randint(jax.random.fold_in(rng, 1), (twos,), 0, 1 << 20) % (slack + 1)
    sizes = sizes.at[1:1 + 2 * twos:2].set(source_of - moved).at[2:2 + 2 * twos:2].set(sink + moved)
    return sizes[jax.random.permutation(jax.random.fold_in(rng, 2), amount)]


def scatter_about(stream_key, shape, scale, most, shards=(), kind=jnp.bfloat16):
    drawn = scale * jax.random.normal(stream_key, shape, jnp.float32)
    if shards:
        drawn = drawn * levels(stream_key, shape, shards, -0.22, 0.18)
    return jnp.clip(drawn, -most, most).astype(kind)


def setup_inputs(seed: int = 0) -> dict:
    splits = jax.random.split(jax.random.key(seed), 12)
    inputs_x = draw_inputs_x(jax.random.fold_in(splits[11], 71), 0)
    gate_z = scatter_about(splits[1], (SEQ, INNER), 1.0, 6.0, ((0, 64), (1, 8)))
    input_b = draw_input_b(jax.random.fold_in(splits[11], 71), 0)
    input_c = draw_input_c(jax.random.fold_in(splits[11], 71), 0)
    dt_raw = draw_dt_raw(jax.random.fold_in(splits[11], 71), 0)
    a_log = draw_a_log(jax.random.fold_in(splits[11], 71), 0)
    dt_bias = jnp.clip(-3.0 + 2.0 * jax.random.uniform(splits[6], (HEADS,), jnp.float32) ** levels(splits[6], (HEADS,), ((0, 8),), -0.2, 0.2), -3.0, -1.0)
    skip_d = jnp.clip(0.5 + 1.0 * jax.random.uniform(splits[7], (HEADS,), jnp.float32) ** levels(splits[7], (HEADS,), ((0, 8),), -0.2, 0.2), 0.5, 1.5)
    norm_gain = jnp.clip(1.0 + 0.18 * jax.random.normal(splits[8], (INNER,), jnp.float32), 0.1, 1.9)
    lengths = ragged(splits[9], DOCS, SEQ - STRETCH, DOC_MOST, 2).astype(jnp.int32)
    cotangent = scatter_about(splits[10], (SEQ, INNER), 1.0, 6.0, ((0, 64), (1, 8)))
    return {"inputs_x": inputs_x, "gate_z": gate_z, "input_b": input_b, "input_c": input_c, "dt_raw": dt_raw, "a_log": a_log, "dt_bias": dt_bias, "skip_d": skip_d, "norm_gain": norm_gain, "lengths": lengths, "cotangent": cotangent}


EPSILON = 1e-05
PRECISE = lax.Precision.HIGHEST

def decay_terms(raw_steps, log_rates, step_bias):
    deltas = jax.nn.softplus(raw_steps + step_bias[None, :])
    return (deltas, -jnp.exp(log_rates)[None, :] * deltas)

def token_flags(lengths, first_place, count, live_end):
    doc_ends = jnp.cumsum(lengths)
    doc_starts = doc_ends - lengths
    places = first_place + jnp.arange(count, dtype=jnp.int32)
    opened = jnp.any(places[:, None] == doc_starts[None, :], axis=1)
    living = places < live_end
    keeping = jnp.where(living & jnp.logical_not(opened), 1.0, 0.0).astype(jnp.float32)
    return (keeping, jnp.where(living, 1.0, 0.0).astype(jnp.float32))

def block_state(signal, input_map, deltas, log_decay, keeping):
    length, head_count, head_width = signal.shape
    group_count = input_map.shape[1]
    resets = jnp.cumsum(1.0 - keeping)
    summed = jnp.cumsum(log_decay, axis=0)
    ending = summed[-1]
    weights = jnp.where((resets == resets[-1])[:, None], jnp.exp(ending[None, :] - summed), 0.0) * deltas
    through = jnp.where(resets[-1] == 0.0, jnp.exp(ending), 0.0)
    scaled = (signal * weights[:, :, None]).reshape(length, group_count, -1, head_width)
    states = jnp.einsum('lgkp,lgn->gkpn', scaled, input_map, precision=PRECISE)
    return (through, states.reshape(head_count, head_width, input_map.shape[2]))

def block_output(signal, input_map, output_map, deltas, log_decay, keeping, entering):
    length, head_count, head_width = signal.shape
    group_count, state_width = (input_map.shape[1], input_map.shape[2])
    resets = jnp.cumsum(1.0 - keeping)
    summed = jnp.cumsum(log_decay, axis=0).T
    places = jnp.arange(length)
    allowed = (places[:, None] >= places[None, :]) & (resets[:, None] == resets[None, :])
    spread = jnp.where(allowed[None], summed[:, :, None] - summed[:, None, :], 0.0)
    decays = jnp.where(allowed[None], jnp.exp(spread), 0.0)
    intersection = jnp.einsum('tgn,sgn->gts', output_map, input_map, precision=PRECISE)
    mixing = decays.reshape(group_count, -1, length, length) * intersection[:, None] * deltas.T.reshape(group_count, -1, 1, length)
    within = jnp.einsum('gkts,sgkp->tgkp', mixing, signal.reshape(length, group_count, -1, head_width), precision=PRECISE)
    carried = jnp.einsum('tgn,gkpn->tgkp', output_map, entering.reshape(group_count, -1, head_width, state_width), precision=PRECISE)
    fresh = jnp.where(resets[:, None] == 0.0, jnp.exp(summed.T), 0.0)
    joined = within + carried * fresh.reshape(length, group_count, -1)[..., None]
    return joined.reshape(length, head_count, head_width)

def reference(inputs_x, gate_z, input_b, input_c, dt_raw, a_log, dt_bias, skip_d, norm_gain, lengths, cotangent):
    count = SEQ // STRETCH
    keeping, living = token_flags(lengths, jnp.int32(0), SEQ, SEQ - STRETCH)
    gate_value = jax.nn.silu(gate_z.astype(jnp.float32))
    pulling = cotangent.astype(jnp.float32)

    def loss(x_float, b_float, c_float, raw_steps, gain_vector):
        deltas, log_decay = decay_terms(raw_steps, a_log, dt_bias)
        pieces = (x_float.reshape(count, STRETCH, HEADS, HEAD_DIM), b_float.reshape(count, STRETCH, GROUPS, STATE), c_float.reshape(count, STRETCH, GROUPS, STATE), deltas.reshape(count, STRETCH, HEADS), log_decay.reshape(count, STRETCH, HEADS), keeping.reshape(count, STRETCH))

        def advance(holding, member):
            signal, in_map, out_map, step_part, decay_part, keep_part = member
            produced = block_output(signal, in_map, out_map, step_part, decay_part, keep_part, holding) + skip_d[None, :, None] * signal
            through, states = block_state(signal, in_map, step_part, decay_part, keep_part)
            return (through[:, None, None] * holding + states, produced)
        start_state = jnp.zeros((HEADS, HEAD_DIM, STATE), jnp.float32)
        _, produced = lax.scan(jax.checkpoint(advance), start_state, pieces)
        core_value = produced.reshape(SEQ, INNER)
        shaped = core_value * gate_value * living[:, None]
        scaling = lax.rsqrt(lax.optimization_barrier(jnp.mean(shaped * shaped, axis=1)) + EPSILON)
        return jnp.sum(shaped * scaling[:, None] * gain_vector[None, :] * pulling)
    grads = jax.grad(loss, argnums=(0, 1, 2, 3, 4))(inputs_x.astype(jnp.float32), input_b.astype(jnp.float32), input_c.astype(jnp.float32), dt_raw, norm_gain)
    return (grads[0].astype(jnp.bfloat16), grads[1].astype(jnp.bfloat16), grads[2].astype(jnp.bfloat16), grads[3], grads[4])
```

```python
import functools

import jax
import jax.numpy as jnp
from jax import lax
from jax.experimental import pallas as pl
from jax.experimental.pallas import tpu as pltpu
from jax.sharding import Mesh
from jax.sharding import PartitionSpec as P

HEAD_DIM = 64
STATE = 128
STRETCH = 128
LANES = 128
QUAD = 4
EPSILON = 1e-05
F32 = jnp.float32
BF16 = jnp.bfloat16
NN = (((1,), (0,)), ((), ()))
NT = (((1,), (1,)), ((), ()))


def mul(a, b, dims=NN):
    return lax.dot_general(a, b, dims, preferred_element_type=F32)


def exact(a, b, dims=NN):
    return lax.dot_general(
        a, b, dims, precision=lax.Precision.HIGHEST, preferred_element_type=F32
    )


def split(a):
    high = a.astype(BF16)
    return (high, (a - high.astype(F32)).astype(BF16))


def mul_sx(a, b, dims=NN):
    return mul(a[0], b, dims) + mul(a[1], b, dims)


def mul_xs(a, b, dims=NN):
    return mul(a, b[0], dims) + mul(a, b[1], dims)


def mul_ss(a, b, dims=NN):
    return mul(a[0], b[0], dims) + (mul(a[0], b[1], dims) + mul(a[1], b[0], dims))


def spread(a, tile):
    rows = a.shape[0]
    lane = lax.broadcasted_iota(jnp.int32, (rows, LANES), 1)
    left = jnp.broadcast_to(a[:, 2 * tile : 2 * tile + 1], (rows, LANES))
    right = jnp.broadcast_to(a[:, 2 * tile + 1 : 2 * tile + 2], (rows, LANES))
    return jnp.where(lane < HEAD_DIM, left, right)


def cols(tile):
    return pl.ds(tile * LANES, LANES)


def head_sums(values, heads):
    total = None
    for tile, value in enumerate(values):
        lane = lax.broadcasted_iota(jnp.int32, (LANES, heads), 0)
        head = lax.broadcasted_iota(jnp.int32, (LANES, heads), 1)
        ones = jnp.where(head == 2 * tile + (lane >= HEAD_DIM).astype(jnp.int32), 1.0, 0.0)
        part = exact(value, ones.astype(F32))
        total = part if total is None else total + part
    return total


def place_marks(info_ref, docs, rows, axis):
    shape = (rows, 1) if axis == 0 else (1, rows)
    first, live_end = info_ref[docs], info_ref[docs + 1]
    places = first + lax.broadcasted_iota(jnp.int32, shape, axis)
    resets = jnp.maximum(places - live_end + 1, 0)
    start = jnp.int32(0)
    for doc in range(docs):
        inside = jnp.where(start >= first, 1, 0)
        resets = resets + jnp.where(places >= start, inside, 0)
        start = start + info_ref[doc]
    return (places < live_end, resets)


def steps(dt_ref, alog_ref, bias_ref, rows):
    raw = dt_ref[...] + bias_ref[...]
    deltas = jnp.maximum(raw, 0.0) + jnp.log1p(jnp.exp(-jnp.abs(raw)))
    log_decay = -jnp.exp(alog_ref[...]) * deltas
    at = lax.broadcasted_iota(jnp.int32, (rows, rows), 0)
    of = lax.broadcasted_iota(jnp.int32, (rows, rows), 1)
    lower = jnp.where(at >= of, 1.0, 0.0).astype(F32)
    return (raw, deltas, exact(lower, log_decay))


def states_kernel(docs, info_ref, x_ref, b_ref, dt_ref, alog_ref, bias_ref, out_ref):
    rows = x_ref.shape[0]
    tiles = x_ref.shape[1] // LANES
    _, resets = place_marks(info_ref, docs, rows, 0)
    _, deltas, summed = steps(dt_ref, alog_ref, bias_ref, rows)
    ending = summed[rows - 1 : rows, :]
    last = resets[rows - 1 : rows, :]
    weights = jnp.where(resets == last, jnp.exp(ending - summed), 0.0) * deltas
    through = jnp.where(last == 0, jnp.exp(ending), 0.0)
    b_turned = b_ref[...].astype(F32).T.astype(BF16)
    per = tiles // QUAD
    for tile in range(tiles):
        weighted = x_ref[:, cols(tile)].astype(F32) * spread(weights, tile)
        part, half = divmod(tile, per)
        out_ref[part, pl.ds(half * STATE, STATE), :] = mul_xs(b_turned, split(weighted))
    for part in range(QUAD):
        out_ref[part, pl.ds(per * STATE, 8), :] = jnp.concatenate(
            [spread(through, part * per + half) for half in range(per)]
            + [jnp.zeros((8 - per, LANES), F32)]
        )


def within_kernel(
    docs, info_ref, x_ref, b_ref, c_ref, dt_ref, alog_ref, bias_ref, skip_ref, out_ref
):
    rows = x_ref.shape[0]
    tiles = x_ref.shape[1] // LANES
    _, resets = place_marks(info_ref, docs, rows, 0)
    _, resets_row = place_marks(info_ref, docs, rows, 1)
    _, deltas, summed = steps(dt_ref, alog_ref, bias_ref, rows)
    middle = summed[rows // 2 - 1 : rows // 2, :]
    rising = jnp.exp(summed - middle)
    falling = jnp.exp(middle - summed) * deltas
    at = lax.broadcasted_iota(jnp.int32, (rows, rows), 0)
    of = lax.broadcasted_iota(jnp.int32, (rows, rows), 1)
    allowed = (at >= of) & (resets == resets_row)
    crossing = split(jnp.where(allowed, mul(c_ref[...], b_ref[...], NT), 0.0))
    skip = skip_ref[...]
    for tile in range(tiles):
        x = x_ref[:, cols(tile)].astype(F32)
        inner = mul_ss(crossing, split(x * spread(falling, tile)))
        out_ref[:, cols(tile)] = inner * spread(rising, tile) + x * spread(skip, tile)


def sigmoid(value):
    return 1.0 / (1.0 + jnp.exp(-value))


def output_kernel(
    docs,
    info_ref,
    within_ref,
    z_ref,
    cot_ref,
    c_ref,
    dt_ref,
    alog_ref,
    bias_ref,
    gain_ref,
    entering_ref,
    core_ref,
    sums_ref,
):
    rows = z_ref.shape[0]
    tiles = z_ref.shape[1] // LANES
    per = tiles // QUAD
    living, resets = place_marks(info_ref, docs, rows, 0)
    _, _, summed = steps(dt_ref, alog_ref, bias_ref, rows)
    fresh = jnp.where(resets == 0, jnp.exp(summed), 0.0)
    c = c_ref[...]
    squares = jnp.zeros((rows, LANES), F32)
    products = jnp.zeros((rows, LANES), F32)
    for tile in range(tiles):
        part, half = divmod(tile, per)
        entering = split(entering_ref[part, pl.ds(half * STATE, STATE), :])
        core = within_ref[:, cols(tile)] + mul_xs(c, entering) * spread(fresh, tile)
        core_ref[:, cols(tile)] = core
        z = z_ref[:, cols(tile)].astype(F32)
        shaped = jnp.where(living, core * (z * sigmoid(z)), 0.0)
        squares += shaped * shaped
        products += gain_ref[:, cols(tile)] * cot_ref[:, cols(tile)].astype(F32) * shaped
    ones = jnp.ones((8, LANES), F32)
    sums_ref[0:1, :] = exact(ones, squares, NT)[0:1]
    sums_ref[1:2, :] = exact(ones, products, NT)[0:1]


def pull_kernel(
    docs,
    channels,
    info_ref,
    core_ref,
    z_ref,
    cot_ref,
    c_ref,
    dt_ref,
    alog_ref,
    bias_ref,
    gain_ref,
    sums_ref,
    pull_ref,
    out_ref,
    gain_out_ref,
):
    rows = z_ref.shape[0]
    tiles = z_ref.shape[1] // LANES
    per = tiles // QUAD
    living, resets = place_marks(info_ref, docs, rows, 0)
    _, _, summed = steps(dt_ref, alog_ref, bias_ref, rows)
    fresh = jnp.where(resets == 0, jnp.exp(summed), 0.0)
    sums = sums_ref[0]
    for other in range(1, sums_ref.shape[0]):
        sums = sums + sums_ref[other]
    scaling_row = lax.rsqrt(sums[0:1] / channels + EPSILON)
    second_row = scaling_row * scaling_row * scaling_row * sums[1:2] / channels
    at = lax.broadcasted_iota(jnp.int32, (rows, rows), 0)
    of = lax.broadcasted_iota(jnp.int32, (rows, rows), 1)
    scaling = jnp.sum(jnp.where(at == of, scaling_row, 0.0), axis=1, keepdims=True)
    second = jnp.sum(jnp.where(at == of, second_row, 0.0), axis=1, keepdims=True)
    c_turned = c_ref[...].astype(F32).T.astype(BF16)
    for tile in range(tiles):
        part, half = divmod(tile, per)
        z = z_ref[:, cols(tile)].astype(F32)
        gate = jnp.where(living, z * sigmoid(z), 0.0)
        shaped = core_ref[:, cols(tile)] * gate
        scaled = cot_ref[:, cols(tile)].astype(F32) * scaling
        gain_out_ref[:, cols(tile)] = jnp.sum(scaled * shaped, axis=0, keepdims=True)
        pulled = (scaled * gain_ref[:, cols(tile)] - second * shaped) * gate
        pull_ref[:, cols(tile)] = pulled
        out_ref[part, pl.ds(half * STATE, STATE), :] = mul_xs(
            c_turned, split(pulled * spread(fresh, tile))
        )
        out_ref[part, pl.ds(per * STATE, 8), :] = jnp.zeros((8, LANES), F32)


def inner_kernel(
    docs,
    info_ref,
    x_ref,
    b_ref,
    c_ref,
    dt_ref,
    alog_ref,
    bias_ref,
    skip_ref,
    core_ref,
    pull_ref,
    entering_ref,
    inner_ref,
    b_out_ref,
    c_out_ref,
    rows_out_ref,
):
    rows = x_ref.shape[0]
    tiles = x_ref.shape[1] // LANES
    per = tiles // QUAD
    _, resets = place_marks(info_ref, docs, rows, 0)
    _, resets_row = place_marks(info_ref, docs, rows, 1)
    _, deltas, summed = steps(dt_ref, alog_ref, bias_ref, rows)
    middle = summed[rows // 2 - 1 : rows // 2, :]
    rising = jnp.exp(summed - middle)
    falling = jnp.exp(middle - summed)
    fresh = jnp.where(resets == 0, jnp.exp(summed), 0.0)
    falling_steps = falling * deltas
    at = lax.broadcasted_iota(jnp.int32, (rows, rows), 0)
    of = lax.broadcasted_iota(jnp.int32, (rows, rows), 1)
    same = resets == resets_row
    b, c = b_ref[...], c_ref[...]
    turned = split(jnp.where((at <= of) & same, mul(b, c, NT), 0.0))
    skip = skip_ref[...]
    paired = jnp.zeros((rows, rows), F32)
    c_sum = jnp.zeros((rows, STATE), F32)
    along = []
    for tile in range(tiles):
        part, half = divmod(tile, per)
        pulled = pull_ref[:, cols(tile)]
        x = x_ref[:, cols(tile)].astype(F32)
        raised = split(pulled * spread(rising, tile))
        inner_ref[:, cols(tile)] = mul_ss(turned, raised) * spread(falling, tile)
        paired += mul_ss(raised, split(x * spread(falling_steps, tile)), NT)
        entering = split(entering_ref[part, pl.ds(half * STATE, STATE), :])
        c_sum += mul_ss(split(pulled * spread(fresh, tile)), entering, NT)
        along.append(pulled * (core_ref[:, cols(tile)] - x * spread(skip, tile)))
    paired = jnp.where((at >= of) & same, paired, 0.0)
    c_out_ref[...] = (c_sum + mul_sx(split(paired), b)).astype(BF16)
    b_out_ref[...] = mul_sx(split(paired.T), c)
    rows_out_ref[...] = head_sums(along, deltas.shape[1])


def final_kernel(
    docs,
    info_ref,
    x_ref,
    b_ref,
    dt_ref,
    alog_ref,
    bias_ref,
    skip_ref,
    pull_ref,
    inner_ref,
    b_in_ref,
    rows_in_ref,
    entering_ref,
    own_ref,
    later_ref,
    x_out_ref,
    b_out_ref,
    dt_out_ref,
):
    rows = x_ref.shape[0]
    tiles = x_ref.shape[1] // LANES
    per = tiles // QUAD
    _, resets = place_marks(info_ref, docs, rows, 0)
    raw, deltas, summed = steps(dt_ref, alog_ref, bias_ref, rows)
    ending = summed[rows - 1 : rows, :]
    last = resets[rows - 1 : rows, :]
    to_end = jnp.where(resets == last, jnp.exp(ending - summed), 0.0)
    weights = to_end * deltas
    b = b_ref[...]
    skip = skip_ref[...]
    b_sum = b_in_ref[...]
    along = []
    ends = []
    for tile in range(tiles):
        part, half = divmod(tile, per)
        place = pl.ds(half * STATE, STATE)
        later_full = later_ref[part, place, :]
        later = split(later_full)
        x = x_ref[:, cols(tile)].astype(F32)
        back = inner_ref[:, cols(tile)] + mul_xs(b, later) * spread(to_end, tile)
        x_out_ref[:, cols(tile)] = (
            back * spread(deltas, tile) + pull_ref[:, cols(tile)] * spread(skip, tile)
        ).astype(BF16)
        b_sum += mul_ss(split(x * spread(weights, tile)), later, NT)
        along.append(x * back)
        through = own_ref[part, pl.ds(per * STATE + half, 1), :]
        leaving = through * entering_ref[part, place, :] + own_ref[part, place, :]
        ends.append(
            jnp.broadcast_to(jnp.sum(later_full * leaving, axis=0, keepdims=True), (8, LANES))
        )
    b_out_ref[...] = b_sum.astype(BF16)
    heads = deltas.shape[1]
    direct = head_sums(along, heads)
    end_pull = head_sums(ends, heads)[0:1]
    at = lax.broadcasted_iota(jnp.int32, (rows, rows), 0)
    of = lax.broadcasted_iota(jnp.int32, (rows, rows), 1)
    upper = jnp.where(at <= of, 1.0, 0.0).astype(F32)
    log_pull = exact(upper, rows_in_ref[...] - direct * deltas) + end_pull
    dt_out_ref[...] = (direct - jnp.exp(alog_ref[...]) * log_pull) * sigmoid(raw)


def gather_kernel(reverse, got_ref, marks_ref, out_ref):
    count = out_ref.shape[0]
    per = out_ref.shape[1] - 8
    halves = (got_ref.shape[1] - 8) // STATE
    piece = per // halves
    order = list(range(QUAD))
    if reverse:
        order.reverse()
    for half in range(halves):
        place = pl.ds(half * STATE, STATE)
        joined = got_ref[order[0], place, :]
        for one in order[1:]:
            through = marks_ref[one, pl.ds(halves * STATE + half, 1), :]
            joined = through * joined + got_ref[one, place, :]
        for to in range(count):
            out_ref[to, pl.ds(half * piece, piece), :] = joined[to * piece : (to + 1) * piece]
    marks = marks_ref[0, pl.ds(halves * STATE, 8), :]
    for one in range(1, QUAD):
        marks = marks * marks_ref[one, pl.ds(halves * STATE, 8), :]
    for to in range(count):
        out_ref[to, pl.ds(per, 8), :] = marks


def along_kernel(reverse, got_ref, marks_ref, out_ref):
    count = got_ref.shape[0]
    per = out_ref.shape[1]
    halves = 2
    piece = per // halves
    order = list(range(count))
    if reverse:
        order.reverse()
    for half in range(halves):
        place = pl.ds(half * piece, piece)
        holding = jnp.zeros((piece, LANES), F32)
        for one in order:
            out_ref[one, place, :] = holding
            through = marks_ref[one, pl.ds(per + half, 1), :]
            holding = through * holding + got_ref[one, place, :]


def hand_kernel(reverse, back_ref, got_ref, marks_ref, out_ref):
    count = back_ref.shape[0]
    halves = out_ref.shape[1] // STATE
    piece = back_ref.shape[1] // halves
    order = list(range(QUAD))
    if reverse:
        order.reverse()
    for half in range(halves):
        place = pl.ds(half * STATE, STATE)
        holding = jnp.concatenate(
            [back_ref[one, pl.ds(half * piece, piece), :] for one in range(count)]
        )
        for one in order:
            out_ref[one, place, :] = holding
            through = marks_ref[one, pl.ds(halves * STATE + half, 1), :]
            holding = through * holding + got_ref[one, place, :]


def call(kernel, outs, *operands, smem=False):
    in_specs = [pl.BlockSpec(memory_space=pltpu.VMEM) for _ in operands]
    if smem:
        in_specs[0] = pl.BlockSpec(memory_space=pltpu.SMEM)
    many = isinstance(outs, (list, tuple))
    spec = pl.BlockSpec(memory_space=pltpu.VMEM)
    return pl.pallas_call(
        kernel,
        out_shape=outs,
        in_specs=in_specs,
        out_specs=[spec] * len(outs) if many else spec,
        compiler_params=pltpu.CompilerParams(vmem_limit_bytes=32 * 1024 * 1024),
    )(*operands)


def like(shape, kind=F32):
    return jax.ShapeDtypeStruct(shape, kind)


def exchange(value, axis):
    return lax.all_to_all(value, axis, 0, 0, tiled=True)


def carry(own, marks, reverse):
    along = lax.axis_size("z")
    halves = (own.shape[1] - 8) // STATE
    per = halves * STATE // along
    got = exchange(own, "x")
    quad_marks = got if marks is None else marks[0]
    joined = call(
        functools.partial(gather_kernel, reverse),
        like((along, per + 8, LANES)),
        got,
        quad_marks,
    )
    pieces = exchange(joined, "z")
    piece_marks = pieces if marks is None else marks[1]
    scanned = call(
        functools.partial(along_kernel, reverse),
        like((along, per, LANES)),
        pieces,
        piece_marks,
    )
    back = exchange(scanned, "z")
    handed = call(
        functools.partial(hand_kernel, reverse),
        like((QUAD, halves * STATE, LANES)),
        back,
        got,
        quad_marks,
    )
    return (exchange(handed, "x"), (quad_marks, piece_marks))


def per_device(
    inputs_x,
    gate_z,
    input_b,
    input_c,
    dt_raw,
    a_log,
    dt_bias,
    skip_d,
    norm_gain,
    lengths,
    cotangent,
):
    rows, width = inputs_x.shape
    docs = lengths.shape[0]
    along = lax.axis_size("z")
    place = lax.axis_index("z") * lax.axis_size("x") + lax.axis_index("x")
    total = rows * lax.axis_size("z") * lax.axis_size("x")
    channels = float(width * lax.axis_size("tensor"))
    info = jnp.concatenate(
        [lengths, jnp.stack([place * rows, jnp.int32(total - STRETCH)]).astype(jnp.int32)]
    )
    a_log, dt_bias, skip_d = a_log[None, :], dt_bias[None, :], skip_d[None, :]
    gain = norm_gain[None, :]
    message = like((QUAD, width // QUAD // LANES * STATE + 8, LANES))
    wide = like((rows, width))

    own = call(
        functools.partial(states_kernel, docs),
        message,
        info,
        inputs_x,
        input_b,
        dt_raw,
        a_log,
        dt_bias,
        smem=True,
    )
    entering, marks = carry(own, None, False)
    within = call(
        functools.partial(within_kernel, docs),
        wide,
        info,
        inputs_x,
        input_b,
        input_c,
        dt_raw,
        a_log,
        dt_bias,
        skip_d,
        smem=True,
    )
    core, sums = call(
        functools.partial(output_kernel, docs),
        [wide, like((2, rows))],
        info,
        within,
        gate_z,
        cotangent,
        input_c,
        dt_raw,
        a_log,
        dt_bias,
        gain,
        entering,
        smem=True,
    )
    sums = lax.all_gather(sums, "tensor")
    pulled, own_back, gain_part = call(
        functools.partial(pull_kernel, docs, channels),
        [wide, message, like((1, width))],
        info,
        core,
        gate_z,
        cotangent,
        input_c,
        dt_raw,
        a_log,
        dt_bias,
        gain,
        sums,
        smem=True,
    )
    grad_gain = exchange(gain_part.reshape(along, QUAD, -1).transpose(1, 0, 2), "x").sum(0)
    grad_gain = exchange(grad_gain, "z").sum(0)
    later, _ = carry(own_back, marks, True)
    inner, b_part, grad_c, rows_part = call(
        functools.partial(inner_kernel, docs),
        [wide, like((rows, STATE)), like((rows, STATE), BF16), like(dt_raw.shape)],
        info,
        inputs_x,
        input_b,
        input_c,
        dt_raw,
        a_log,
        dt_bias,
        skip_d,
        core,
        pulled,
        entering,
        smem=True,
    )
    grad_x, grad_b, grad_dt = call(
        functools.partial(final_kernel, docs),
        [like((rows, width), BF16), like((rows, STATE), BF16), like(dt_raw.shape)],
        info,
        inputs_x,
        input_b,
        dt_raw,
        a_log,
        dt_bias,
        skip_d,
        pulled,
        inner,
        b_part,
        rows_part,
        entering,
        own,
        later,
        smem=True,
    )
    return (grad_x, grad_b, grad_c, grad_dt, grad_gain)


def solution(mesh):
    count = mesh.devices.shape[0]
    split_mesh = Mesh(
        mesh.devices.reshape(count // QUAD, QUAD, mesh.devices.shape[1]), ("z", "x", "tensor")
    )
    tokens = ("z", "x")
    both = P(tokens, "tensor")
    return jax.shard_map(
        per_device,
        mesh=split_mesh,
        in_specs=(
            both,
            both,
            both,
            both,
            both,
            P("tensor"),
            P("tensor"),
            P("tensor"),
            P("tensor"),
            P(),
            both,
        ),
        out_specs=(both, both, both, both, P(("tensor", "z", "x"))),
        check_vma=False,
    )
```

```python
import functools

import jax
import jax.numpy as jnp
from jax import lax
from jax.experimental import pallas as pl
from jax.experimental.pallas import tpu as pltpu
from jax.sharding import Mesh
from jax.sharding import PartitionSpec as P

HEAD_DIM = 64
STATE = 128
STRETCH = 128
LANES = 128
WIDE = 2 * LANES
GROUP = 8
EPSILON = 1e-05
F32 = jnp.float32
BF16 = jnp.bfloat16
NN = (((1,), (0,)), ((), ()))
NT = (((1,), (1,)), ((), ()))


def mul(a, b, dims=NN):
    return lax.dot_general(a, b, dims, preferred_element_type=F32)


def split(a):
    high = a.astype(BF16)
    return (high, (a - high.astype(F32)).astype(BF16))


def mul_sx(a, b, dims=NN):
    return mul(a[0], b, dims) + mul(a[1], b, dims)


def mul_xs(a, b, dims=NN):
    return mul(a, b[0], dims) + mul(a, b[1], dims)


def mul_ss(a, b, dims=NN):
    return mul(a[0], b[0], dims) + (mul(a[0], b[1], dims) + mul(a[1], b[0], dims))


def mul_3x(a, b, dims=NN):
    high = a.astype(BF16)
    rest = a - high.astype(F32)
    middle = rest.astype(BF16)
    low = (rest - middle.astype(F32)).astype(BF16)
    return mul(high, b, dims) + (mul(middle, b, dims) + mul(low, b, dims))


def spread(a, pair):
    rows = a.shape[0]
    lane = lax.broadcasted_iota(jnp.int32, (rows, LANES), 1)
    tiles = []
    for one in (4 * pair, 4 * pair + 2):
        left = jnp.broadcast_to(a[:, one : one + 1], (rows, LANES))
        right = jnp.broadcast_to(a[:, one + 1 : one + 2], (rows, LANES))
        tiles.append(jnp.where(lane < HEAD_DIM, left, right))
    return jnp.concatenate(tiles, axis=1)


def cols(pair):
    return pl.ds(pair * WIDE, WIDE)


def two_tiles(ref, pair, place):
    return jnp.concatenate([ref[2 * pair, place, :], ref[2 * pair + 1, place, :]], axis=1)


def head_marks(heads, pair):
    head = lax.broadcasted_iota(jnp.int32, (heads, WIDE), 0)
    lane = lax.broadcasted_iota(jnp.int32, (heads, WIDE), 1)
    start = (head - 4 * pair) * HEAD_DIM
    return jnp.where((lane >= start) & (lane < start + HEAD_DIM), 1.0, 0.0).astype(BF16)


def ordered(rows):
    at = lax.broadcasted_iota(jnp.int32, (rows, rows), 0)
    of = lax.broadcasted_iota(jnp.int32, (rows, rows), 1)
    return (at, of)


def place_marks(info_ref, docs, rows, axis):
    shape = (rows, 1) if axis == 0 else (1, rows)
    first, live_end = info_ref[docs], info_ref[docs + 1]
    places = first + lax.broadcasted_iota(jnp.int32, shape, axis)
    resets = jnp.maximum(places - live_end + 1, 0)
    start = jnp.int32(0)
    for doc in range(docs):
        inside = jnp.where(start >= first, 1, 0)
        resets = resets + jnp.where(places >= start, inside, 0)
        start = start + info_ref[doc]
    return (places < live_end, resets)


def softplus(value):
    return jnp.maximum(value, 0.0) + jnp.log1p(jnp.exp(-jnp.abs(value)))


def sigmoid(value):
    return 1.0 / (1.0 + jnp.exp(-value))


def states_kernel(
    docs, info_ref, x_ref, b_ref, dt_ref, alog_ref, bias_ref, out_ref, summed_ref, deltas_ref
):
    rows = x_ref.shape[0]
    pairs = x_ref.shape[1] // WIDE
    _, resets = place_marks(info_ref, docs, rows, 0)
    at, of = ordered(rows)
    deltas_row = softplus(dt_ref[...] + bias_ref[...])
    before = jnp.where(at <= of, 1.0, 0.0).astype(BF16)
    summed = mul_3x(-jnp.exp(alog_ref[...]) * deltas_row, before).T
    deltas = deltas_row.T
    summed_ref[...] = summed
    deltas_ref[...] = deltas
    ending = summed[rows - 1 : rows, :]
    last = resets[rows - 1 : rows, :]
    weights = jnp.where(resets == last, jnp.exp(ending - summed), 0.0) * deltas
    through = jnp.broadcast_to(jnp.where(last == 0, jnp.exp(ending), 0.0), (8, deltas.shape[1]))
    b_turned = b_ref[...].astype(F32).T.astype(BF16)
    for pair in range(pairs):
        weighted = x_ref[:, cols(pair)].astype(F32) * spread(weights, pair)
        state = mul_xs(b_turned, split(weighted))
        marks = spread(through, pair)
        for half in range(2):
            lanes = slice(half * LANES, (half + 1) * LANES)
            out_ref[2 * pair + half, 0:STATE, :] = state[:, lanes]
            out_ref[2 * pair + half, STATE : STATE + 8, :] = marks[:, lanes]


def within_kernel(
    docs,
    info_ref,
    x_ref,
    z_ref,
    cot_ref,
    b_ref,
    c_ref,
    summed_ref,
    deltas_ref,
    skip_ref,
    out_ref,
    fresh_ref,
    gate_ref,
    gated_ref,
):
    rows = x_ref.shape[0]
    pairs = x_ref.shape[1] // WIDE
    living, resets = place_marks(info_ref, docs, rows, 0)
    _, resets_row = place_marks(info_ref, docs, rows, 1)
    deltas, summed = deltas_ref[...], summed_ref[...]
    middle = summed[rows // 2 - 1 : rows // 2, :]
    rising = jnp.exp(summed - middle)
    falling = jnp.exp(middle - summed) * deltas
    fresh = jnp.where(resets == 0, jnp.exp(summed), 0.0)
    at, of = ordered(rows)
    allowed = (at >= of) & (resets == resets_row)
    crossing = split(jnp.where(allowed, mul(c_ref[...], b_ref[...], NT), 0.0))
    skip = skip_ref[...]
    for pair in range(pairs):
        x = x_ref[:, cols(pair)].astype(F32)
        inner = mul_ss(crossing, split(x * spread(falling, pair)))
        out_ref[:, cols(pair)] = inner * spread(rising, pair) + x * spread(skip, pair)
        fresh_ref[:, cols(pair)] = spread(fresh, pair)
        z = z_ref[:, cols(pair)].astype(F32)
        gate = jnp.where(living, z * sigmoid(z), 0.0)
        gate_ref[:, cols(pair)] = gate
        gated_ref[:, cols(pair)] = gate * cot_ref[:, cols(pair)].astype(F32)


def output_kernel(
    within_ref,
    fresh_ref,
    gate_ref,
    gated_ref,
    c_ref,
    gain_ref,
    entering_ref,
    core_ref,
    bent_ref,
    sums_ref,
):
    rows, width = within_ref.shape
    c = c_ref[...]
    c_twice = jnp.concatenate([c, c], axis=1)
    squares = jnp.zeros((rows, WIDE), F32)
    products = jnp.zeros((rows, WIDE), F32)
    for pair in range(width // WIDE):
        entering = split(two_tiles(entering_ref, pair, slice(None)))
        carried = mul(c_twice, jnp.concatenate(entering, axis=0))
        core = within_ref[:, cols(pair)] + carried * fresh_ref[:, cols(pair)]
        core_ref[:, cols(pair)] = core
        gate = gate_ref[:, cols(pair)]
        shaped = core * gate
        bent_ref[:, cols(pair)] = shaped * gate
        squares += shaped * shaped
        products += gain_ref[:, cols(pair)] * (gated_ref[:, cols(pair)] * core)
    ones = jnp.ones((8, WIDE), BF16)
    for row, total in enumerate((squares, products)):
        high, low = split(total)
        rest = (total - high.astype(F32) - low.astype(F32)).astype(BF16)
        sum_row = mul(ones, high, NT) + (mul(ones, low, NT) + mul(ones, rest, NT))
        sums_ref[row : row + 1, :] = sum_row[0:1]


def pull_kernel(
    channels,
    core_ref,
    bent_ref,
    gated_ref,
    fresh_ref,
    c_ref,
    gain_ref,
    sums_ref,
    pull_ref,
    out_ref,
):
    rows, width = core_ref.shape
    sums = sums_ref[0]
    for other in range(1, sums_ref.shape[0]):
        sums = sums + sums_ref[other]
    scaling_row = lax.rsqrt(sums[0:1] / channels + EPSILON)
    second_row = scaling_row * scaling_row * scaling_row * sums[1:2] / channels
    at, of = ordered(rows)
    scaling = jnp.sum(jnp.where(at == of, scaling_row, 0.0), axis=1, keepdims=True)
    second = jnp.sum(jnp.where(at == of, second_row, 0.0), axis=1, keepdims=True)
    c_turned = c_ref[...].astype(F32).T.astype(BF16)
    gains = []
    for pair in range(width // WIDE):
        scaled = gated_ref[:, cols(pair)] * scaling
        gain_sum = jnp.sum(scaled * core_ref[:, cols(pair)], axis=0, keepdims=True)
        gains += [gain_sum[:, :LANES], gain_sum[:, LANES:]]
        pulled = scaled * gain_ref[:, cols(pair)] - second * bent_ref[:, cols(pair)]
        pull_ref[:, cols(pair)] = pulled
        state = mul_xs(c_turned, split(pulled * fresh_ref[:, cols(pair)]))
        out_ref[2 * pair, 0:STATE, :] = state[:, :LANES]
        out_ref[2 * pair + 1, 0:STATE, :] = state[:, LANES:]
    for member in range(GROUP):
        for one in range(GROUP):
            out_ref[member, STATE + one : STATE + one + 1, :] = gains[one]


def inner_kernel(
    docs,
    info_ref,
    x_ref,
    b_ref,
    c_ref,
    summed_ref,
    deltas_ref,
    skip_ref,
    core_ref,
    pull_ref,
    fresh_ref,
    entering_ref,
    own_ref,
    base_ref,
    weights_ref,
    leaving_ref,
    b_out_ref,
    c_out_ref,
    along_ref,
    back_ref,
):
    rows = x_ref.shape[0]
    pairs = x_ref.shape[1] // WIDE
    _, resets = place_marks(info_ref, docs, rows, 0)
    _, resets_row = place_marks(info_ref, docs, rows, 1)
    deltas, summed = deltas_ref[...], summed_ref[...]
    heads = deltas.shape[1]
    middle = summed[rows // 2 - 1 : rows // 2, :]
    rising = jnp.exp(summed - middle)
    falling = jnp.exp(middle - summed) * deltas
    ending = summed[rows - 1 : rows, :]
    last = resets[rows - 1 : rows, :]
    weights = jnp.where(resets == last, jnp.exp(ending - summed), 0.0) * deltas
    at, of = ordered(rows)
    same = resets == resets_row
    b, c = b_ref[...], c_ref[...]
    turned = split(jnp.where((at <= of) & same, mul(b, c, NT), 0.0))
    skip = skip_ref[...]
    paired = jnp.zeros((rows, rows), F32)
    c_sum = jnp.zeros((rows, STATE), F32)
    along = jnp.zeros((heads, rows), F32)
    back = jnp.zeros((heads, rows), F32)
    for pair in range(pairs):
        pulled = pull_ref[:, cols(pair)]
        x = x_ref[:, cols(pair)].astype(F32)
        raised = split(pulled * spread(rising, pair))
        lowered = spread(falling, pair)
        direct = mul_ss(turned, raised) * lowered
        skipped = spread(skip, pair)
        base_ref[:, cols(pair)] = direct + skipped * pulled
        weights_ref[:, cols(pair)] = spread(weights, pair)
        paired += mul_ss(raised, split(x * lowered), NT)
        entering = two_tiles(entering_ref, pair, slice(None))
        c_sum += mul_ss(split(pulled * fresh_ref[:, cols(pair)]), split(entering), NT)
        marks = head_marks(heads, pair)
        along += mul_xs(marks, split(pulled * (core_ref[:, cols(pair)] - x * skipped)), NT)
        back += mul_xs(marks, split(x * direct), NT)
        through = two_tiles(own_ref, pair, slice(STATE, STATE + 1))
        leaving = through * entering + two_tiles(own_ref, pair, slice(0, STATE))
        leaving_ref[:, cols(pair)] = leaving
    paired = jnp.where((at >= of) & same, paired, 0.0)
    c_out_ref[...] = (c_sum + mul_sx(split(paired), b)).astype(BF16)
    b_out_ref[...] = mul_sx(split(paired.T), c)
    along_ref[...] = along
    back_ref[...] = back


def final_kernel(
    x_ref,
    b_ref,
    dt_ref,
    alog_ref,
    bias_ref,
    base_ref,
    weights_ref,
    leaving_ref,
    b_in_ref,
    along_ref,
    back_ref,
    later_ref,
    x_out_ref,
    b_out_ref,
    dt_out_ref,
):
    rows = x_ref.shape[0]
    heads = dt_ref.shape[0]
    b = b_ref[...]
    b_twice = jnp.concatenate([b, b], axis=1)
    b_sum = b_in_ref[...]
    back = back_ref[...]
    ends = jnp.zeros((heads, 8), F32)
    for pair in range(x_ref.shape[1] // WIDE):
        later_full = two_tiles(later_ref, pair, slice(None))
        later = split(later_full)
        weights = weights_ref[:, cols(pair)]
        gained = mul(b_twice, jnp.concatenate(later, axis=0)) * weights
        x_out_ref[:, cols(pair)] = (base_ref[:, cols(pair)] + gained).astype(BF16)
        x = x_ref[:, cols(pair)].astype(F32)
        b_sum += mul_ss(split(x * weights), later, NT)
        marks = head_marks(heads, pair)
        back += mul_xs(marks, split(x * gained), NT)
        end = jnp.sum(later_full * leaving_ref[:, cols(pair)], axis=0, keepdims=True)
        ends += mul_xs(marks, split(jnp.broadcast_to(end, (8, WIDE))), NT)
    b_out_ref[...] = b_sum.astype(BF16)
    at, of = ordered(rows)
    after = jnp.where(at >= of, 1.0, 0.0).astype(BF16)
    log_pull = mul_3x(along_ref[...] - back, after) + ends[:, 0:1]
    raw = dt_ref[...] + bias_ref[...]
    direct = back / softplus(raw)
    dt_out_ref[...] = (direct - jnp.exp(alog_ref[...]) * log_pull) * sigmoid(raw)


def gather_kernel(reverse, got_ref, marks_ref, out_ref, rest_ref):
    order = list(range(GROUP))
    if reverse:
        order.reverse()
    joined = got_ref[order[0], 0:STATE, :]
    rest = got_ref[0, STATE : STATE + 8, :]
    marks = marks_ref[0, STATE : STATE + 8, :]
    for one in order[1:]:
        joined = marks_ref[one, STATE : STATE + 1, :] * joined + got_ref[one, 0:STATE, :]
    for one in range(1, GROUP):
        rest = rest + got_ref[one, STATE : STATE + 8, :]
        marks = marks * marks_ref[one, STATE : STATE + 8, :]
    out_ref[0:STATE, :] = joined
    out_ref[STATE : STATE + 8, :] = marks
    rest_ref[...] = rest


def join_kernel(own_ref, got_ref, out_ref):
    through = own_ref[STATE : STATE + 1, :]
    out_ref[0:STATE, :] = own_ref[0:STATE, :] + through * got_ref[0:STATE, :]
    out_ref[STATE : STATE + 8, :] = (
        own_ref[STATE : STATE + 8, :] * got_ref[STATE : STATE + 8, :]
    )


def hand_kernel(reverse, near_ref, far_ref, got_ref, marks_ref, out_ref):
    order = list(range(GROUP))
    if reverse:
        order.reverse()
    holding = near_ref[0:STATE, :] + near_ref[STATE : STATE + 1, :] * far_ref[0:STATE, :]
    for one in order:
        out_ref[one] = holding
        if one != order[-1]:
            through = marks_ref[one, STATE : STATE + 1, :]
            holding = through * holding + got_ref[one, 0:STATE, :]


def call(kernel, outs, *operands, smem=False):
    in_specs = [pl.BlockSpec(memory_space=pltpu.VMEM) for _ in operands]
    if smem:
        in_specs[0] = pl.BlockSpec(memory_space=pltpu.SMEM)
    many = isinstance(outs, (list, tuple))
    spec = pl.BlockSpec(memory_space=pltpu.VMEM)
    return pl.pallas_call(
        kernel,
        out_shape=outs,
        in_specs=in_specs,
        out_specs=[spec] * len(outs) if many else spec,
        compiler_params=pltpu.CompilerParams(vmem_limit_bytes=32 * 1024 * 1024),
    )(*operands)


def like(shape, kind=F32):
    return jax.ShapeDtypeStruct(shape, kind)


def exchange(value):
    return lax.all_to_all(value, ("zl", "x"), 0, 0, tiled=True)


def moved(value, by):
    count = lax.axis_size("zh")
    pairs = [(i, i + by) for i in range(count) if 0 <= i + by < count]
    return lax.ppermute(value, "zh", pairs) if pairs else jnp.zeros_like(value)


def swapped(value, bit):
    count = lax.axis_size("zh")
    if bit >= count:
        return jnp.zeros_like(value)
    return lax.ppermute(value, "zh", [(i, i ^ bit) for i in range(count)])


def carry(own, marks, beside):
    reverse = marks is not None
    way = -1 if reverse else 1
    got = exchange(own)
    if not reverse:
        marks = got
    joined, rest = call(
        functools.partial(gather_kernel, reverse),
        [like(own.shape[1:]), like((8, LANES))],
        got,
        marks,
    )
    from_next = moved(joined, way)
    beside = beside()
    if reverse:
        rest = rest + swapped(rest, 4)
    from_next, rest, beside = lax.optimization_barrier((from_next, rest, beside))
    twice = call(join_kernel, like(own.shape[1:]), joined, from_next)
    near, far = moved(twice, way), moved(twice, 3 * way)
    if reverse:
        rest = rest + swapped(rest, 2)
    handed = call(
        functools.partial(hand_kernel, reverse),
        like((GROUP, STATE, LANES)),
        near,
        far,
        got,
        marks,
    )
    return (exchange(handed), marks, rest, beside)


def per_device(
    inputs_x,
    gate_z,
    input_b,
    input_c,
    dt_raw,
    a_log,
    dt_bias,
    skip_d,
    norm_gain,
    lengths,
    cotangent,
):
    rows, width = inputs_x.shape
    heads = dt_raw.shape[1]
    docs = lengths.shape[0]
    member = lax.axis_index(("zl", "x"))
    group = lax.axis_index("zh")
    total = rows * lax.axis_size("zh") * GROUP
    channels = float(width * lax.axis_size("tensor"))
    first = (group * GROUP + member) * rows
    info = jnp.concatenate(
        [lengths, jnp.stack([first, jnp.int32(total - STRETCH)]).astype(jnp.int32)]
    )
    steps = dt_raw.T
    a_log, dt_bias = a_log[:, None], dt_bias[:, None]
    skip_d, gain = skip_d[None, :], norm_gain[None, :]
    message = like((GROUP, STATE + 8, LANES))
    wide = like((rows, width))
    small = like((rows, heads))
    turned = like((heads, rows))

    own, summed, deltas = call(
        functools.partial(states_kernel, docs),
        [message, small, small],
        info,
        inputs_x,
        input_b,
        steps,
        a_log,
        dt_bias,
        smem=True,
    )

    def before():
        return call(
            functools.partial(within_kernel, docs),
            [wide, wide, wide, wide],
            info,
            inputs_x,
            gate_z,
            cotangent,
            input_b,
            input_c,
            summed,
            deltas,
            skip_d,
            smem=True,
        )

    entering, marks, _, (within, fresh, gate, gated) = carry(own, None, before)
    core, bent, sums = call(
        output_kernel,
        [wide, wide, like((2, rows))],
        within,
        fresh,
        gate,
        gated,
        input_c,
        gain,
        entering,
    )
    sums = lax.all_gather(sums, "tensor")
    pulled, own_back = call(
        functools.partial(pull_kernel, channels),
        [wide, message],
        core,
        bent,
        gated,
        fresh,
        input_c,
        gain,
        sums,
    )

    def after():
        return call(
            functools.partial(inner_kernel, docs),
            [
                wide,
                wide,
                like((STATE, width)),
                like((rows, STATE)),
                like((rows, STATE), BF16),
                turned,
                turned,
            ],
            info,
            inputs_x,
            input_b,
            input_c,
            summed,
            deltas,
            skip_d,
            core,
            pulled,
            fresh,
            entering,
            own,
            smem=True,
        )

    later, _, gain_sum, beside = carry(own_back, marks, after)
    base, weights, leaving, b_part, grad_c, along, back = beside
    grad_x, grad_b, grad_dt = call(
        final_kernel,
        [like((rows, width), BF16), like((rows, STATE), BF16), turned],
        inputs_x,
        input_b,
        steps,
        a_log,
        dt_bias,
        base,
        weights,
        leaving,
        b_part,
        along,
        back,
        later,
    )
    gain_sum = gain_sum + swapped(gain_sum, 1)
    share = width // (GROUP * lax.axis_size("zh"))
    grad_gain = lax.dynamic_slice(gain_sum, (group, member * share), (1, share))[0]
    return (grad_x, grad_b, grad_c, grad_dt.T, grad_gain)


def solution(mesh):
    count, across = mesh.devices.shape
    split_mesh = Mesh(
        mesh.devices.reshape(count // GROUP, 2, GROUP // 2, across), ("zh", "zl", "x", "tensor")
    )
    tokens = ("zh", "zl", "x")
    both = P(tokens, "tensor")
    alone = P("tensor")
    return jax.shard_map(
        per_device,
        mesh=split_mesh,
        in_specs=(both, both, both, both, both, alone, alone, alone, alone, P(), both),
        out_specs=(both, both, both, both, P(("tensor", "zh", "zl", "x"))),
        check_vma=False,
    )
```

```python
import functools

import jax
import jax.numpy as jnp
from jax import lax
from jax.experimental import pallas as pl
from jax.experimental.pallas import tpu as pltpu
from jax.sharding import Mesh
from jax.sharding import PartitionSpec as P

HEAD_DIM = 64
STATE = 128
STRETCH = 128
LANES = 128
WIDE = 2 * LANES
GROUP = 8
EPSILON = 1e-05
F32 = jnp.float32
BF16 = jnp.bfloat16
NN = (((1,), (0,)), ((), ()))
NT = (((1,), (1,)), ((), ()))


def mul(a, b, dims=NN):
    return lax.dot_general(a, b, dims, preferred_element_type=F32)


def split(a):
    high = a.astype(BF16)
    return (high, (a - high.astype(F32)).astype(BF16))


def mul_sx(a, b, dims=NN):
    return mul(a[0], b, dims) + mul(a[1], b, dims)


def mul_xs(a, b, dims=NN):
    return mul(a, b[0], dims) + mul(a, b[1], dims)


def mul_ss(a, b, dims=NN):
    return mul(a[0], b[0], dims) + (mul(a[0], b[1], dims) + mul(a[1], b[0], dims))


def mul_3x(a, b, dims=NN):
    high = a.astype(BF16)
    rest = a - high.astype(F32)
    middle = rest.astype(BF16)
    low = (rest - middle.astype(F32)).astype(BF16)
    return mul(high, b, dims) + (mul(middle, b, dims) + mul(low, b, dims))


def spread(a, pair):
    rows = a.shape[0]
    lane = lax.broadcasted_iota(jnp.int32, (rows, LANES), 1)
    tiles = []
    for one in (4 * pair, 4 * pair + 2):
        left = jnp.broadcast_to(a[:, one : one + 1], (rows, LANES))
        right = jnp.broadcast_to(a[:, one + 1 : one + 2], (rows, LANES))
        tiles.append(jnp.where(lane < HEAD_DIM, left, right))
    return jnp.concatenate(tiles, axis=1)


def cols(pair):
    return pl.ds(pair * WIDE, WIDE)


def two_tiles(ref, pair, place):
    return jnp.concatenate([ref[2 * pair, place, :], ref[2 * pair + 1, place, :]], axis=1)


def head_marks(heads, pair):
    head = lax.broadcasted_iota(jnp.int32, (heads, WIDE), 0)
    lane = lax.broadcasted_iota(jnp.int32, (heads, WIDE), 1)
    start = (head - 4 * pair) * HEAD_DIM
    return jnp.where((lane >= start) & (lane < start + HEAD_DIM), 1.0, 0.0).astype(BF16)


def ordered(rows):
    at = lax.broadcasted_iota(jnp.int32, (rows, rows), 0)
    of = lax.broadcasted_iota(jnp.int32, (rows, rows), 1)
    return (at, of)


def member_index():
    return lax.axis_index("zl") * lax.axis_size("x") + lax.axis_index("x")


def place_marks(lengths_ref, rows, axis):
    shape = (rows, 1) if axis == 0 else (1, rows)
    docs = lengths_ref.shape[0]
    first = (lax.axis_index("zh") * GROUP + member_index()) * rows
    live_end = rows * GROUP * lax.axis_size("zh") - STRETCH
    places = first + lax.broadcasted_iota(jnp.int32, shape, axis)
    resets = jnp.maximum(places - live_end + 1, 0)
    start = jnp.int32(0)
    for doc in range(docs):
        inside = jnp.where(start >= first, 1, 0)
        resets = resets + jnp.where(places >= start, inside, 0)
        start = start + lengths_ref[doc]
    return (places < live_end, resets)


def softplus(value):
    return jnp.maximum(value, 0.0) + jnp.log1p(jnp.exp(-jnp.abs(value)))


def sigmoid(value):
    return 1.0 / (1.0 + jnp.exp(-value))


def column(row):
    at, of = ordered(row.shape[1])
    return jnp.sum(jnp.where(at == of, row, 0.0), axis=1, keepdims=True)


def states_kernel(
    lengths_ref,
    x_hbm,
    b_hbm,
    dt_hbm,
    alog_hbm,
    bias_hbm,
    out_ref,
    summed_ref,
    deltas_ref,
    x_ref,
    b_ref,
    dt_ref,
    alog_ref,
    bias_ref,
    sems,
):
    sources = (alog_hbm, bias_hbm, dt_hbm, b_hbm, x_hbm)
    targets = (alog_ref, bias_ref, dt_ref, b_ref, x_ref)
    copies = [
        pltpu.make_async_copy(source, target, sems.at[one])
        for one, (source, target) in enumerate(zip(sources, targets))
    ]
    for copy in copies:
        copy.start()
    rows = x_ref.shape[0]
    pairs = x_ref.shape[1] // WIDE
    _, resets = place_marks(lengths_ref, rows, 0)
    at, of = ordered(rows)
    before = jnp.where(at <= of, 1.0, 0.0).astype(BF16)
    for copy in copies[:3]:
        copy.wait()
    deltas_row = softplus(dt_ref[...] + column(bias_ref[...]))
    summed = mul_3x(-jnp.exp(column(alog_ref[...])) * deltas_row, before).T
    deltas = deltas_row.T
    summed_ref[...] = summed
    deltas_ref[...] = deltas
    ending = summed[rows - 1 : rows, :]
    last = resets[rows - 1 : rows, :]
    weights = jnp.where(resets == last, jnp.exp(ending - summed), 0.0) * deltas
    through = jnp.broadcast_to(jnp.where(last == 0, jnp.exp(ending), 0.0), (8, deltas.shape[1]))
    copies[3].wait()
    b_turned = b_ref[...].astype(F32).T.astype(BF16)
    copies[4].wait()
    for pair in range(pairs):
        weighted = x_ref[:, cols(pair)].astype(F32) * spread(weights, pair)
        state = mul_xs(b_turned, split(weighted))
        marks = spread(through, pair)
        for half in range(2):
            lanes = slice(half * LANES, (half + 1) * LANES)
            out_ref[2 * pair + half, 0:STATE, :] = state[:, lanes]
            out_ref[2 * pair + half, STATE : STATE + 8, :] = marks[:, lanes]


def within_kernel(
    lengths_ref,
    x_ref,
    z_ref,
    cot_ref,
    b_ref,
    c_ref,
    summed_ref,
    deltas_ref,
    skip_ref,
    out_ref,
    fresh_ref,
    gate_ref,
    gated_ref,
):
    rows = x_ref.shape[0]
    pairs = x_ref.shape[1] // WIDE
    living, resets = place_marks(lengths_ref, rows, 0)
    _, resets_row = place_marks(lengths_ref, rows, 1)
    deltas, summed = deltas_ref[...], summed_ref[...]
    middle = summed[rows // 2 - 1 : rows // 2, :]
    rising = jnp.exp(summed - middle)
    falling = jnp.exp(middle - summed) * deltas
    fresh = jnp.where(resets == 0, jnp.exp(summed), 0.0)
    at, of = ordered(rows)
    allowed = (at >= of) & (resets == resets_row)
    crossing = split(jnp.where(allowed, mul(c_ref[...], b_ref[...], NT), 0.0))
    skip = skip_ref[...]
    for pair in range(pairs):
        x = x_ref[:, cols(pair)].astype(F32)
        inner = mul_ss(crossing, split(x * spread(falling, pair)))
        out_ref[:, cols(pair)] = inner * spread(rising, pair) + x * spread(skip, pair)
        fresh_ref[:, cols(pair)] = spread(fresh, pair)
        z = z_ref[:, cols(pair)].astype(F32)
        gate = jnp.where(living, z * sigmoid(z), 0.0)
        gate_ref[:, cols(pair)] = gate
        gated_ref[:, cols(pair)] = gate * cot_ref[:, cols(pair)].astype(F32)


def output_kernel(
    within_ref,
    fresh_ref,
    gate_ref,
    gated_ref,
    c_ref,
    gain_ref,
    entering_ref,
    core_ref,
    bent_ref,
    sums_ref,
):
    rows, width = within_ref.shape
    c = c_ref[...]
    c_twice = jnp.concatenate([c, c], axis=1)
    squares = jnp.zeros((rows, WIDE), F32)
    products = jnp.zeros((rows, WIDE), F32)
    for pair in range(width // WIDE):
        entering = split(two_tiles(entering_ref, pair, slice(None)))
        carried = mul(c_twice, jnp.concatenate(entering, axis=0))
        core = within_ref[:, cols(pair)] + carried * fresh_ref[:, cols(pair)]
        core_ref[:, cols(pair)] = core
        gate = gate_ref[:, cols(pair)]
        shaped = core * gate
        bent_ref[:, cols(pair)] = shaped * gate
        squares += shaped * shaped
        products += gain_ref[:, cols(pair)] * (gated_ref[:, cols(pair)] * core)
    ones = jnp.ones((8, WIDE), BF16)
    for row, total in enumerate((squares, products)):
        high, low = split(total)
        rest = (total - high.astype(F32) - low.astype(F32)).astype(BF16)
        sum_row = mul(ones, high, NT) + (mul(ones, low, NT) + mul(ones, rest, NT))
        for half in range(2):
            line = 2 * row + half
            for to in range(sums_ref.shape[0]):
                sums_ref[to, line : line + 1, :] = sum_row[0:1, half * LANES : (half + 1) * LANES]


def pull_kernel(
    channels,
    core_ref,
    bent_ref,
    gated_ref,
    fresh_ref,
    c_ref,
    gain_ref,
    sums_ref,
    pull_ref,
    out_ref,
):
    rows, width = core_ref.shape
    sums = sums_ref[0]
    for other in range(1, sums_ref.shape[0]):
        sums = sums + sums_ref[other]
    squares = jnp.concatenate([sums[0:1], sums[1:2]], axis=1)
    products = jnp.concatenate([sums[2:3], sums[3:4]], axis=1)
    scaling_row = lax.rsqrt(squares / channels + EPSILON)
    second_row = scaling_row * scaling_row * scaling_row * products / channels
    scaling = column(scaling_row)
    second = column(second_row)
    c_turned = c_ref[...].astype(F32).T.astype(BF16)
    gains = []
    for pair in range(width // WIDE):
        scaled = gated_ref[:, cols(pair)] * scaling
        gain_sum = jnp.sum(scaled * core_ref[:, cols(pair)], axis=0, keepdims=True)
        gains += [gain_sum[:, :LANES], gain_sum[:, LANES:]]
        pulled = scaled * gain_ref[:, cols(pair)] - second * bent_ref[:, cols(pair)]
        pull_ref[:, cols(pair)] = pulled
        state = mul_xs(c_turned, split(pulled * fresh_ref[:, cols(pair)]))
        out_ref[2 * pair, 0:STATE, :] = state[:, :LANES]
        out_ref[2 * pair + 1, 0:STATE, :] = state[:, LANES:]
    for member in range(GROUP):
        for one in range(GROUP):
            out_ref[member, STATE + one : STATE + one + 1, :] = gains[one]


def inner_kernel(
    lengths_ref,
    x_ref,
    b_ref,
    c_ref,
    summed_ref,
    deltas_ref,
    skip_ref,
    core_ref,
    pull_ref,
    fresh_ref,
    entering_ref,
    own_ref,
    base_ref,
    weights_ref,
    leaving_ref,
    b_out_ref,
    c_out_ref,
    along_ref,
    back_ref,
):
    rows = x_ref.shape[0]
    pairs = x_ref.shape[1] // WIDE
    _, resets = place_marks(lengths_ref, rows, 0)
    _, resets_row = place_marks(lengths_ref, rows, 1)
    deltas, summed = deltas_ref[...], summed_ref[...]
    heads = deltas.shape[1]
    middle = summed[rows // 2 - 1 : rows // 2, :]
    rising = jnp.exp(summed - middle)
    falling = jnp.exp(middle - summed) * deltas
    ending = summed[rows - 1 : rows, :]
    last = resets[rows - 1 : rows, :]
    weights = jnp.where(resets == last, jnp.exp(ending - summed), 0.0) * deltas
    at, of = ordered(rows)
    same = resets == resets_row
    b, c = b_ref[...], c_ref[...]
    turned = split(jnp.where((at <= of) & same, mul(b, c, NT), 0.0))
    skip = skip_ref[...]
    paired = jnp.zeros((rows, rows), F32)
    c_sum = jnp.zeros((rows, STATE), F32)
    along = jnp.zeros((heads, rows), F32)
    back = jnp.zeros((heads, rows), F32)
    for pair in range(pairs):
        pulled = pull_ref[:, cols(pair)]
        x = x_ref[:, cols(pair)].astype(F32)
        raised = split(pulled * spread(rising, pair))
        lowered = spread(falling, pair)
        direct = mul_ss(turned, raised) * lowered
        skipped = spread(skip, pair)
        base_ref[:, cols(pair)] = direct + skipped * pulled
        weights_ref[:, cols(pair)] = spread(weights, pair)
        paired += mul_ss(raised, split(x * lowered), NT)
        entering = two_tiles(entering_ref, pair, slice(None))
        c_sum += mul_ss(split(pulled * fresh_ref[:, cols(pair)]), split(entering), NT)
        marks = head_marks(heads, pair)
        along += mul_xs(marks, split(pulled * (core_ref[:, cols(pair)] - x * skipped)), NT)
        back += mul_xs(marks, split(x * direct), NT)
        through = two_tiles(own_ref, pair, slice(STATE, STATE + 1))
        leaving = through * entering + two_tiles(own_ref, pair, slice(0, STATE))
        leaving_ref[:, cols(pair)] = leaving
    paired = jnp.where((at >= of) & same, paired, 0.0)
    c_out_ref[...] = (c_sum + mul_sx(split(paired), b)).astype(BF16)
    b_out_ref[...] = mul_sx(split(paired.T), c)
    along_ref[...] = along
    back_ref[...] = back


def final_kernel(
    x_ref,
    b_ref,
    dt_ref,
    alog_ref,
    bias_ref,
    base_ref,
    weights_ref,
    leaving_ref,
    b_in_ref,
    along_ref,
    back_ref,
    later_ref,
    x_out_ref,
    b_out_ref,
    dt_out_ref,
):
    rows = x_ref.shape[0]
    heads = dt_ref.shape[0]
    b = b_ref[...]
    b_twice = jnp.concatenate([b, b], axis=1)
    b_sum = b_in_ref[...]
    back = back_ref[...]
    ends = jnp.zeros((heads, 8), F32)
    for pair in range(x_ref.shape[1] // WIDE):
        later_full = two_tiles(later_ref, pair, slice(None))
        later = split(later_full)
        weights = weights_ref[:, cols(pair)]
        gained = mul(b_twice, jnp.concatenate(later, axis=0)) * weights
        x_out_ref[:, cols(pair)] = (base_ref[:, cols(pair)] + gained).astype(BF16)
        x = x_ref[:, cols(pair)].astype(F32)
        b_sum += mul_ss(split(x * weights), later, NT)
        marks = head_marks(heads, pair)
        back += mul_xs(marks, split(x * gained), NT)
        end = jnp.sum(later_full * leaving_ref[:, cols(pair)], axis=0, keepdims=True)
        ends += mul_xs(marks, split(jnp.broadcast_to(end, (8, WIDE))), NT)
    b_out_ref[...] = b_sum.astype(BF16)
    at, of = ordered(rows)
    after = jnp.where(at >= of, 1.0, 0.0).astype(BF16)
    log_pull = mul_3x(along_ref[...] - back, after) + ends[:, 0:1]
    raw = dt_ref[...] + column(bias_ref[...])
    direct = back / softplus(raw)
    dt_out_ref[...] = (direct - jnp.exp(column(alog_ref[...])) * log_pull) * sigmoid(raw)


def gather_kernel(reverse, got_ref, marks_ref, out_ref, *gain_ref):
    order = list(range(GROUP))
    if reverse:
        order.reverse()
    joined = got_ref[order[0], 0:STATE, :]
    marks = marks_ref[0, STATE : STATE + 8, :]
    for one in order[1:]:
        joined = marks_ref[one, STATE : STATE + 1, :] * joined + got_ref[one, 0:STATE, :]
    for one in range(1, GROUP):
        marks = marks * marks_ref[one, STATE : STATE + 8, :]
    end = out_ref.shape[0] - 8
    out_ref[0:STATE, :] = joined
    out_ref[end : end + 8, :] = marks
    if reverse:
        gain = got_ref[0, STATE : STATE + 8, :]
        for one in range(1, GROUP):
            gain = gain + got_ref[one, STATE : STATE + 8, :]
        out_ref[STATE : STATE + 8, :] = gain
        gain_ref[0][...] = gain


def join_kernel(reverse, own_ref, got_ref, *refs):
    end = own_ref.shape[0] - 8
    through = own_ref[end : end + 1, :]
    joined = own_ref[0:STATE, :] + through * got_ref[0:STATE, :]
    if reverse:
        gain_ref, gain_got_ref, out_ref, far_ref, gain_out_ref = refs
        both = own_ref[STATE : STATE + 8, :] + got_ref[STATE : STATE + 8, :]
        out_ref[STATE : STATE + 8, :] = both
        far_ref[STATE : STATE + 8, :] = both
        gain_out_ref[...] = gain_ref[...] + gain_got_ref[...]
    else:
        out_ref, far_ref = refs
    out_ref[0:STATE, :] = joined
    far_ref[0:STATE, :] = joined
    out_ref[end : end + 8, :] = own_ref[end : end + 8, :] * got_ref[end : end + 8, :]


def hand_kernel(reverse, near_ref, far_ref, got_ref, marks_ref, *refs):
    order = list(range(GROUP))
    out_ref = refs[-2] if reverse else refs[-1]
    end = near_ref.shape[0] - 8
    holding = near_ref[0:STATE, :] + near_ref[end : end + 1, :] * far_ref[0:STATE, :]
    if reverse:
        order.reverse()
        group = lax.axis_index("zh")
        holding = jnp.where(group == lax.axis_size("zh") - 1, 0.0, holding)
    for one in order:
        out_ref[one] = holding
        if one != order[-1]:
            through = marks_ref[one, STATE : STATE + 1, :]
            holding = through * holding + got_ref[one, 0:STATE, :]
    if reverse:
        table = refs[0][...] + refs[1][...]
        table = table + near_ref[STATE : STATE + 8, :] + far_ref[STATE : STATE + 8, :]
        row = lax.broadcasted_iota(jnp.int32, table.shape, 0)
        table = jnp.where(row == group, table, 0.0)
        gain_ref = refs[-1]
        share = gain_ref.shape[1]
        lane = lax.broadcasted_iota(jnp.int32, (LANES, share), 0)
        place = lax.broadcasted_iota(jnp.int32, (LANES, share), 1)
        chosen = jnp.where(lane == place + share * member_index(), 1.0, 0.0).astype(BF16)
        gain_ref[...] = jnp.sum(mul_3x(table, chosen), axis=0, keepdims=True)


def call(kernel, outs, *operands, smem=False, hbm=False, scratch=()):
    in_specs = [pl.BlockSpec(memory_space=pltpu.HBM if hbm else pltpu.VMEM) for _ in operands]
    if smem:
        in_specs[0] = pl.BlockSpec(memory_space=pltpu.SMEM)
    many = isinstance(outs, (list, tuple))
    spec = pl.BlockSpec(memory_space=pltpu.VMEM)
    return pl.pallas_call(
        kernel,
        out_shape=outs,
        in_specs=in_specs,
        out_specs=[spec] * len(outs) if many else spec,
        scratch_shapes=scratch,
        compiler_params=pltpu.CompilerParams(vmem_limit_bytes=16 * 1024 * 1024),
    )(*operands)


def like(shape, kind=F32):
    return jax.ShapeDtypeStruct(shape, kind)


def exchange(value, axes):
    return lax.all_to_all(value, axes, 0, 0, tiled=True)


def moved(value, by, around):
    count = lax.axis_size("zh")
    pairs = [(i, i + by) for i in range(count)]
    if around:
        pairs = [(i, j % count) for i, j in pairs]
    return lax.ppermute(value, "zh", [(i, j) for i, j in pairs if 0 <= j < count])


def carry(own, beside):
    got = exchange(own, ("zl", "x"))
    message, tile = like(own.shape[1:]), like((STATE, LANES))
    joined = call(functools.partial(gather_kernel, False), message, got, got)
    from_next = moved(joined, 1, False)
    from_next, beside = lax.optimization_barrier((from_next, beside()))
    twice, state = call(
        functools.partial(join_kernel, False), [message, tile], joined, from_next
    )
    handed = call(
        functools.partial(hand_kernel, False),
        like((GROUP, STATE, LANES)),
        moved(twice, 1, False),
        moved(state, 3, False),
        got,
        got,
    )
    return (exchange(handed, ("zl", "x")), got, beside)


def carry_back(own, marks, share, beside):
    got = exchange(own, ("zl", "x"))
    message, table = like((STATE + 16, LANES)), like((8, LANES))
    joined, gain = call(functools.partial(gather_kernel, True), [message, table], got, marks)
    from_next = moved(joined, -1, True)
    gain_next = moved(gain, 1, True)
    from_next, gain_next, beside = lax.optimization_barrier((from_next, gain_next, beside()))
    twice, state, gain = call(
        functools.partial(join_kernel, True),
        [message, like((STATE + 8, LANES)), table],
        joined,
        from_next,
        gain,
        gain_next,
    )
    near, far = moved(twice, -1, True), moved(state, -3, True)
    handed, gain = call(
        functools.partial(hand_kernel, True),
        [like((GROUP, STATE, LANES)), like((1, share))],
        near,
        far,
        got,
        marks,
        gain,
        moved(gain, 2, True),
    )
    return (exchange(handed, ("zl", "x")), gain[0], beside)


def per_device(
    inputs_x,
    gate_z,
    input_b,
    input_c,
    dt_raw,
    a_log,
    dt_bias,
    skip_d,
    norm_gain,
    lengths,
    cotangent,
):
    rows, width = inputs_x.shape
    heads = dt_raw.shape[1]
    channels = float(width * lax.axis_size("tensor"))
    steps = dt_raw.T
    a_log, dt_bias = a_log[None, :], dt_bias[None, :]
    skip_d, gain = skip_d[None, :], norm_gain[None, :]
    message = like((GROUP, STATE + 8, LANES))
    wide = like((rows, width))
    small = like((rows, heads))
    turned = like((heads, rows))

    own, summed, deltas = call(
        states_kernel,
        [message, small, small],
        lengths,
        inputs_x,
        input_b,
        steps,
        a_log,
        dt_bias,
        smem=True,
        hbm=True,
        scratch=[
            pltpu.VMEM(inputs_x.shape, BF16),
            pltpu.VMEM(input_b.shape, BF16),
            pltpu.VMEM(steps.shape, F32),
            pltpu.VMEM(a_log.shape, F32),
            pltpu.VMEM(dt_bias.shape, F32),
            pltpu.SemaphoreType.DMA((5,)),
        ],
    )

    def before():
        return call(
            within_kernel,
            [wide, wide, wide, wide],
            lengths,
            inputs_x,
            gate_z,
            cotangent,
            input_b,
            input_c,
            summed,
            deltas,
            skip_d,
            smem=True,
        )

    entering, marks, (within, fresh, gate, gated) = carry(own, before)
    core, bent, sums = call(
        output_kernel,
        [wide, wide, like((lax.axis_size("tensor"), 2 * rows // LANES, LANES))],
        within,
        fresh,
        gate,
        gated,
        input_c,
        gain,
        entering,
    )
    sums = exchange(sums, "tensor")
    pulled, own_back = call(
        functools.partial(pull_kernel, channels),
        [wide, message],
        core,
        bent,
        gated,
        fresh,
        input_c,
        gain,
        sums,
    )

    def after():
        return call(
            inner_kernel,
            [
                wide,
                wide,
                like((STATE, width)),
                like((rows, STATE)),
                like((rows, STATE), BF16),
                turned,
                turned,
            ],
            lengths,
            inputs_x,
            input_b,
            input_c,
            summed,
            deltas,
            skip_d,
            core,
            pulled,
            fresh,
            entering,
            own,
            smem=True,
        )

    share = width // (GROUP * lax.axis_size("zh"))
    later, grad_gain, beside = carry_back(own_back, marks, share, after)
    base, weights, leaving, b_part, grad_c, along, back = beside
    grad_x, grad_b, grad_dt = call(
        final_kernel,
        [like((rows, width), BF16), like((rows, STATE), BF16), turned],
        inputs_x,
        input_b,
        steps,
        a_log,
        dt_bias,
        base,
        weights,
        leaving,
        b_part,
        along,
        back,
        later,
    )
    return (grad_x, grad_b, grad_c, grad_dt.T, grad_gain)


def solution(mesh):
    count, across = mesh.devices.shape
    split_mesh = Mesh(
        mesh.devices.reshape(count // GROUP, 2, GROUP // 2, across), ("zh", "zl", "x", "tensor")
    )
    tokens = ("zh", "zl", "x")
    both = P(tokens, "tensor")
    alone = P("tensor")
    return jax.shard_map(
        per_device,
        mesh=split_mesh,
        in_specs=(both, both, both, both, both, alone, alone, alone, alone, P(), both),
        out_specs=(both, both, both, both, P(("tensor", "zh", "zl", "x"))),
        check_vma=False,
    )
```

```python
import functools

import jax
import jax.numpy as jnp
from jax import lax
from jax.experimental import pallas as pl
from jax.experimental.pallas import tpu as pltpu
from jax.sharding import Mesh
from jax.sharding import PartitionSpec as P

HEAD_DIM = 64
STATE = 128
STRETCH = 128
LANES = 128
WIDE = 2 * LANES
GROUP = 8
EPSILON = 1e-05
ROOM = 62
F32 = jnp.float32
BF16 = jnp.bfloat16
NN = (((1,), (0,)), ((), ()))
NT = (((1,), (1,)), ((), ()))


def mul(a, b, dims=NN):
    return lax.dot_general(a, b, dims, preferred_element_type=F32)


def split(a):
    high = a.astype(BF16)
    return (high, (a - high.astype(F32)).astype(BF16))


def mul_sx(a, b, dims=NN):
    return mul(a[0], b, dims) + mul(a[1], b, dims)


def mul_xs(a, b, dims=NN):
    return mul(a, b[0], dims) + mul(a, b[1], dims)


def mul_ss(a, b, dims=NN):
    return mul(a[0], b[0], dims) + (mul(a[0], b[1], dims) + mul(a[1], b[0], dims))


def mul_3x(a, b, dims=NN):
    high = a.astype(BF16)
    rest = a - high.astype(F32)
    middle = rest.astype(BF16)
    low = (rest - middle.astype(F32)).astype(BF16)
    return mul(high, b, dims) + (mul(middle, b, dims) + mul(low, b, dims))


def spread(a, pair):
    rows = a.shape[0]
    lane = lax.broadcasted_iota(jnp.int32, (rows, LANES), 1)
    tiles = []
    for one in (4 * pair, 4 * pair + 2):
        left = jnp.broadcast_to(a[:, one : one + 1], (rows, LANES))
        right = jnp.broadcast_to(a[:, one + 1 : one + 2], (rows, LANES))
        tiles.append(jnp.where(lane < HEAD_DIM, left, right))
    return jnp.concatenate(tiles, axis=1)


def cols(pair):
    return pl.ds(pair * WIDE, WIDE)


def two_tiles(ref, pair, place):
    return jnp.concatenate([ref[2 * pair, place, :], ref[2 * pair + 1, place, :]], axis=1)


def head_marks(heads, pair):
    head = lax.broadcasted_iota(jnp.int32, (heads, WIDE), 0)
    lane = lax.broadcasted_iota(jnp.int32, (heads, WIDE), 1)
    start = (head - 4 * pair) * HEAD_DIM
    return jnp.where((lane >= start) & (lane < start + HEAD_DIM), 1.0, 0.0).astype(BF16)


def ordered(rows):
    at = lax.broadcasted_iota(jnp.int32, (rows, rows), 0)
    of = lax.broadcasted_iota(jnp.int32, (rows, rows), 1)
    return (at, of)


def member_index():
    return lax.axis_index("zl") * lax.axis_size("x") + lax.axis_index("x")


def place_marks(lengths_ref, rows, axis):
    shape = (rows, 1) if axis == 0 else (1, rows)
    docs = lengths_ref.shape[0]
    first = (lax.axis_index("zh") * GROUP + member_index()) * rows
    live_end = rows * GROUP * lax.axis_size("zh") - STRETCH
    places = first + lax.broadcasted_iota(jnp.int32, shape, axis)
    resets = jnp.maximum(places - live_end + 1, 0)
    start = jnp.int32(0)
    for doc in range(docs):
        inside = jnp.where(start >= first, 1, 0)
        resets = resets + jnp.where(places >= start, inside, 0)
        start = start + lengths_ref[doc]
    return (places < live_end, resets)


def softplus(value):
    return jnp.maximum(value, 0.0) + jnp.log1p(jnp.exp(-jnp.abs(value)))


def sigmoid(value):
    return 1.0 / (1.0 + jnp.exp(-value))


def column(row):
    at, of = ordered(row.shape[1])
    return jnp.sum(jnp.where(at == of, row, 0.0), axis=1, keepdims=True)


def states_kernel(
    lengths_ref,
    x_hbm,
    b_hbm,
    dt_hbm,
    alog_hbm,
    bias_hbm,
    out_ref,
    summed_ref,
    deltas_ref,
    x_ref,
    b_ref,
    dt_ref,
    alog_ref,
    bias_ref,
    sems,
):
    sources = (alog_hbm, bias_hbm, dt_hbm, b_hbm, x_hbm)
    targets = (alog_ref, bias_ref, dt_ref, b_ref, x_ref)
    copies = [
        pltpu.make_async_copy(source, target, sems.at[one])
        for one, (source, target) in enumerate(zip(sources, targets))
    ]
    for copy in copies:
        copy.start()
    rows = x_ref.shape[0]
    pairs = x_ref.shape[1] // WIDE
    _, resets = place_marks(lengths_ref, rows, 0)
    at, of = ordered(rows)
    before = jnp.where(at <= of, 1.0, 0.0).astype(BF16)
    for copy in copies[:3]:
        copy.wait()
    deltas_row = softplus(dt_ref[...] + column(bias_ref[...]))
    summed = mul_3x(-jnp.exp(column(alog_ref[...])) * deltas_row, before).T
    deltas = deltas_row.T
    summed_ref[...] = summed
    deltas_ref[...] = deltas
    ending = summed[rows - 1 : rows, :]
    last = resets[rows - 1 : rows, :]
    weights = jnp.where(resets == last, jnp.exp(ending - summed), 0.0) * deltas
    through = jnp.broadcast_to(jnp.where(last == 0, jnp.exp(ending), 0.0), (8, deltas.shape[1]))
    copies[3].wait()
    b_turned = b_ref[...].astype(F32).T.astype(BF16)
    copies[4].wait()
    for pair in range(pairs):
        weighted = x_ref[:, cols(pair)].astype(F32) * spread(weights, pair)
        state = mul_xs(b_turned, split(weighted))
        marks = spread(through, pair)
        for half in range(2):
            lanes = slice(half * LANES, (half + 1) * LANES)
            out_ref[2 * pair + half, 0:STATE, :] = state[:, lanes]
            out_ref[2 * pair + half, STATE : STATE + 8, :] = marks[:, lanes]


def within_kernel(
    lengths_ref,
    x_ref,
    z_ref,
    cot_ref,
    b_ref,
    c_ref,
    summed_ref,
    deltas_ref,
    skip_ref,
    out_ref,
    fresh_ref,
    gate_ref,
    gated_ref,
):
    rows = x_ref.shape[0]
    pairs = x_ref.shape[1] // WIDE
    living, resets = place_marks(lengths_ref, rows, 0)
    _, resets_row = place_marks(lengths_ref, rows, 1)
    deltas, summed = deltas_ref[...], summed_ref[...]
    middle = summed[rows // 2 - 1 : rows // 2, :]
    rising = jnp.exp(summed - middle)
    falling = jnp.exp(middle - summed) * deltas
    fresh = jnp.where(resets == 0, jnp.exp(summed), 0.0)
    at, of = ordered(rows)
    allowed = (at >= of) & (resets == resets_row)
    crossing = split(jnp.where(allowed, mul(c_ref[...], b_ref[...], NT), 0.0))
    skip = skip_ref[...]
    for pair in range(pairs):
        x = x_ref[:, cols(pair)].astype(F32)
        inner = mul_ss(crossing, split(x * spread(falling, pair)))
        out_ref[:, cols(pair)] = inner * spread(rising, pair) + x * spread(skip, pair)
        fresh_ref[:, cols(pair)] = spread(fresh, pair)
        z = z_ref[:, cols(pair)].astype(F32)
        gate = jnp.where(living, z * sigmoid(z), 0.0)
        gate_ref[:, cols(pair)] = gate
        gated_ref[:, cols(pair)] = gate * cot_ref[:, cols(pair)].astype(F32)


def output_kernel(
    within_ref,
    fresh_ref,
    gate_ref,
    gated_ref,
    c_ref,
    gain_ref,
    entering_ref,
    core_ref,
    bent_ref,
    sums_ref,
):
    rows, width = within_ref.shape
    c = c_ref[...]
    c_twice = jnp.concatenate([c, c], axis=1)
    squares = jnp.zeros((rows, WIDE), F32)
    products = jnp.zeros((rows, WIDE), F32)
    for pair in range(width // WIDE):
        entering = split(two_tiles(entering_ref, pair, slice(None)))
        carried = mul(c_twice, jnp.concatenate(entering, axis=0))
        core = within_ref[:, cols(pair)] + carried * fresh_ref[:, cols(pair)]
        core_ref[:, cols(pair)] = core
        gate = gate_ref[:, cols(pair)]
        shaped = core * gate
        bent_ref[:, cols(pair)] = shaped * gate
        squares += shaped * shaped
        products += gain_ref[:, cols(pair)] * (gated_ref[:, cols(pair)] * core)
    ones = jnp.ones((8, WIDE), BF16)
    for row, total in enumerate((squares, products)):
        high, low = split(total)
        rest = (total - high.astype(F32) - low.astype(F32)).astype(BF16)
        sum_row = mul(ones, high, NT) + (mul(ones, low, NT) + mul(ones, rest, NT))
        for half in range(2):
            line = 2 * row + half
            for to in range(sums_ref.shape[0]):
                sums_ref[to, line : line + 1, :] = sum_row[0:1, half * LANES : (half + 1) * LANES]


def pull_kernel(
    channels,
    core_ref,
    bent_ref,
    gated_ref,
    fresh_ref,
    c_ref,
    gain_ref,
    sums_ref,
    pull_ref,
    out_ref,
):
    rows, width = core_ref.shape
    sums = sums_ref[0]
    for other in range(1, sums_ref.shape[0]):
        sums = sums + sums_ref[other]
    squares = jnp.concatenate([sums[0:1], sums[1:2]], axis=1)
    products = jnp.concatenate([sums[2:3], sums[3:4]], axis=1)
    scaling_row = lax.rsqrt(squares / channels + EPSILON)
    second_row = scaling_row * scaling_row * scaling_row * products / channels
    scaling = column(scaling_row)
    second = column(second_row)
    c_turned = c_ref[...].astype(F32).T.astype(BF16)
    gains = []
    for pair in range(width // WIDE):
        scaled = gated_ref[:, cols(pair)] * scaling
        gain_sum = jnp.sum(scaled * core_ref[:, cols(pair)], axis=0, keepdims=True)
        gains += [gain_sum[:, :LANES], gain_sum[:, LANES:]]
        pulled = scaled * gain_ref[:, cols(pair)] - second * bent_ref[:, cols(pair)]
        pull_ref[:, cols(pair)] = pulled
        state = mul_xs(c_turned, split(pulled * fresh_ref[:, cols(pair)]))
        out_ref[2 * pair, 0:STATE, :] = state[:, :LANES]
        out_ref[2 * pair + 1, 0:STATE, :] = state[:, LANES:]
    for member in range(GROUP):
        for one in range(GROUP):
            out_ref[member, STATE + one : STATE + one + 1, :] = gains[one]


def inner_kernel(
    lengths_ref,
    x_ref,
    b_ref,
    c_ref,
    summed_ref,
    deltas_ref,
    skip_ref,
    core_ref,
    pull_ref,
    fresh_ref,
    entering_ref,
    own_ref,
    base_ref,
    weights_ref,
    leaving_ref,
    b_out_ref,
    c_out_ref,
    along_ref,
    back_ref,
):
    rows = x_ref.shape[0]
    pairs = x_ref.shape[1] // WIDE
    _, resets = place_marks(lengths_ref, rows, 0)
    _, resets_row = place_marks(lengths_ref, rows, 1)
    deltas, summed = deltas_ref[...], summed_ref[...]
    heads = deltas.shape[1]
    middle = summed[rows // 2 - 1 : rows // 2, :]
    rising = jnp.exp(summed - middle)
    falling = jnp.exp(middle - summed) * deltas
    ending = summed[rows - 1 : rows, :]
    last = resets[rows - 1 : rows, :]
    weights = jnp.where(resets == last, jnp.exp(ending - summed), 0.0) * deltas
    at, of = ordered(rows)
    same = resets == resets_row
    b, c = b_ref[...], c_ref[...]
    turned = split(jnp.where((at <= of) & same, mul(b, c, NT), 0.0))
    skip = skip_ref[...]
    paired = jnp.zeros((rows, rows), F32)
    c_sum = jnp.zeros((rows, STATE), F32)
    along = jnp.zeros((heads, rows), F32)
    back = jnp.zeros((heads, rows), F32)
    for pair in range(pairs):
        pulled = pull_ref[:, cols(pair)]
        x = x_ref[:, cols(pair)].astype(F32)
        raised = split(pulled * spread(rising, pair))
        lowered = spread(falling, pair)
        direct = mul_ss(turned, raised) * lowered
        skipped = spread(skip, pair)
        base_ref[:, cols(pair)] = direct + skipped * pulled
        weights_ref[:, cols(pair)] = spread(weights, pair)
        paired += mul_ss(raised, split(x * lowered), NT)
        entering = two_tiles(entering_ref, pair, slice(None))
        c_sum += mul_ss(split(pulled * fresh_ref[:, cols(pair)]), split(entering), NT)
        marks = head_marks(heads, pair)
        along += mul_xs(marks, split(pulled * (core_ref[:, cols(pair)] - x * skipped)), NT)
        back += mul_xs(marks, split(x * direct), NT)
        through = two_tiles(own_ref, pair, slice(STATE, STATE + 1))
        leaving = through * entering + two_tiles(own_ref, pair, slice(0, STATE))
        leaving_ref[:, cols(pair)] = leaving
    paired = jnp.where((at >= of) & same, paired, 0.0)
    c_out_ref[...] = (c_sum + mul_sx(split(paired), b)).astype(BF16)
    b_out_ref[...] = mul_sx(split(paired.T), c)
    along_ref[...] = along
    back_ref[...] = back


def final_kernel(
    x_ref,
    b_ref,
    dt_ref,
    alog_ref,
    bias_ref,
    base_ref,
    weights_ref,
    leaving_ref,
    b_in_ref,
    along_ref,
    back_ref,
    later_ref,
    gains_ref,
    x_out_ref,
    b_out_ref,
    dt_out_ref,
    gain_out_ref,
):
    rows = x_ref.shape[0]
    heads = dt_ref.shape[0]
    table = gains_ref[0]
    for one in range(1, gains_ref.shape[0]):
        table = table + gains_ref[one]
    table = jnp.broadcast_to(table, (8, LANES))
    share = gain_out_ref.shape[1]
    lane = lax.broadcasted_iota(jnp.int32, (LANES, share), 0)
    place = lax.broadcasted_iota(jnp.int32, (LANES, share), 1)
    chosen = jnp.where(lane == place + share * member_index(), 1.0, 0.0).astype(BF16)
    gain_out_ref[...] = mul_3x(table, chosen)[0:1]
    b = b_ref[...]
    b_twice = jnp.concatenate([b, b], axis=1)
    b_sum = b_in_ref[...]
    back = back_ref[...]
    ends = jnp.zeros((heads, 8), F32)
    for pair in range(x_ref.shape[1] // WIDE):
        later_full = two_tiles(later_ref, pair, slice(None))
        later = split(later_full)
        weights = weights_ref[:, cols(pair)]
        gained = mul(b_twice, jnp.concatenate(later, axis=0)) * weights
        x_out_ref[:, cols(pair)] = (base_ref[:, cols(pair)] + gained).astype(BF16)
        x = x_ref[:, cols(pair)].astype(F32)
        b_sum += mul_ss(split(x * weights), later, NT)
        marks = head_marks(heads, pair)
        back += mul_xs(marks, split(x * gained), NT)
        end = jnp.sum(later_full * leaving_ref[:, cols(pair)], axis=0, keepdims=True)
        ends += mul_xs(marks, split(jnp.broadcast_to(end, (8, WIDE))), NT)
    b_out_ref[...] = b_sum.astype(BF16)
    at, of = ordered(rows)
    after = jnp.where(at >= of, 1.0, 0.0).astype(BF16)
    log_pull = mul_3x(along_ref[...] - back, after) + ends[:, 0:1]
    raw = dt_ref[...] + column(bias_ref[...])
    direct = back / softplus(raw)
    dt_out_ref[...] = (direct - jnp.exp(column(alog_ref[...])) * log_pull) * sigmoid(raw)


def gather_kernel(reverse, got_ref, marks_ref, out_ref, *gain_ref):
    order = list(range(GROUP))
    if reverse:
        order.reverse()
    joined = got_ref[order[0], 0:STATE, :]
    marks = marks_ref[0, STATE : STATE + 8, :]
    for one in order[1:]:
        joined = marks_ref[one, STATE : STATE + 1, :] * joined + got_ref[one, 0:STATE, :]
    for one in range(1, GROUP):
        marks = marks * marks_ref[one, STATE : STATE + 8, :]
    end = out_ref.shape[0] - 8
    out_ref[0:STATE, :] = joined
    out_ref[end : end + 8, :] = marks
    if reverse:
        gain = got_ref[0, STATE : STATE + 8, :]
        for one in range(1, GROUP):
            gain = gain + got_ref[one, STATE : STATE + 8, :]
        gain_ref[0][...] = gain


def join_kernel(own_ref, got_ref, out_ref, far_ref):
    through = own_ref[STATE : STATE + 1, :]
    joined = own_ref[0:STATE, :] + through * got_ref[0:STATE, :]
    out_ref[0:STATE, :] = joined
    far_ref[0:STATE, :] = joined
    out_ref[STATE : STATE + 8, :] = own_ref[STATE : STATE + 8, :] * got_ref[STATE : STATE + 8, :]


def hand_members(holding, reverse, got_ref, marks_ref, out_ref):
    order = list(range(GROUP))
    if reverse:
        order.reverse()
    for one in order:
        out_ref[one] = holding
        if one != order[-1]:
            through = marks_ref[one, STATE : STATE + 1, :]
            holding = through * holding + got_ref[one, 0:STATE, :]


def hand_kernel(reverse, near_ref, far_ref, got_ref, marks_ref, out_ref):
    through = near_ref[STATE : STATE + 1, :]
    holding = near_ref[0:STATE, :] + through * far_ref[0:STATE, :]
    hand_members(holding, reverse, got_ref, marks_ref, out_ref)


def call(kernel, outs, *operands, smem=False, hbm=False, scratch=(), room=16):
    space = pltpu.HBM if hbm else pltpu.VMEM
    in_specs = [jax.tree.map(lambda _: pl.BlockSpec(memory_space=space), one) for one in operands]
    if smem:
        in_specs[0] = pl.BlockSpec(memory_space=pltpu.SMEM)
    many = isinstance(outs, (list, tuple))
    spec = pl.BlockSpec(memory_space=pltpu.VMEM)
    return pl.pallas_call(
        kernel,
        out_shape=outs,
        in_specs=in_specs,
        out_specs=[spec] * len(outs) if many else spec,
        scratch_shapes=scratch,
        compiler_params=pltpu.CompilerParams(vmem_limit_bytes=room * 1024 * 1024),
    )(*operands)


def like(shape, kind=F32):
    return jax.ShapeDtypeStruct(shape, kind)


def exchange(value, axes):
    return lax.all_to_all(value, axes, 0, 0, tiled=True)


def moved(value, by, around):
    count = lax.axis_size("zh")
    pairs = [(i, i + by) for i in range(count)]
    if around:
        pairs = [(i, j % count) for i, j in pairs]
    return lax.ppermute(value, "zh", [(i, j) for i, j in pairs if 0 <= j < count])


def carry(own, beside):
    got = exchange(own, ("zl", "x"))
    message, tile = like(own.shape[1:]), like((STATE, LANES))
    joined = call(functools.partial(gather_kernel, False), message, got, got)
    from_next = moved(joined, 1, False)
    from_next, beside = lax.optimization_barrier((from_next, beside()))
    twice, state = call(join_kernel, [message, tile], joined, from_next)
    handed = call(
        functools.partial(hand_kernel, False),
        like((GROUP, STATE, LANES)),
        moved(twice, 1, False),
        moved(state, 3, False),
        got,
        got,
    )
    return (exchange(handed, ("zl", "x")), got, beside)


def carry_back(own, marks, beside):
    got = exchange(own, ("zl", "x"))
    message, table, tile = like((STATE + 8, LANES)), like((8, LANES)), like((STATE, LANES))
    joined, gain = call(functools.partial(gather_kernel, True), [message, table], got, marks)
    gains = exchange(gain[:, None, :], "zh")
    from_next, beside = lax.optimization_barrier((moved(joined, -1, False), beside()))
    twice, state = call(join_kernel, [message, tile], joined, from_next)
    near, far = moved(twice, -1, False), moved(state, -3, False)
    near, far, gains = lax.optimization_barrier((near, far, gains))
    handed = call(
        functools.partial(hand_kernel, True),
        like((GROUP, STATE, LANES)),
        near,
        far,
        got,
        marks,
    )
    return (exchange(handed, ("zl", "x")), gains, beside)


def per_device(
    inputs_x,
    gate_z,
    input_b,
    input_c,
    dt_raw,
    a_log,
    dt_bias,
    skip_d,
    norm_gain,
    lengths,
    cotangent,
):
    rows, width = inputs_x.shape
    heads = dt_raw.shape[1]
    channels = float(width * lax.axis_size("tensor"))
    steps = dt_raw.T
    a_log, dt_bias = a_log[None, :], dt_bias[None, :]
    skip_d, gain = skip_d[None, :], norm_gain[None, :]
    message = like((GROUP, STATE + 8, LANES))
    wide = like((rows, width))
    small = like((rows, heads))
    turned = like((heads, rows))

    own, summed, deltas = call(
        states_kernel,
        [message, small, small],
        lengths,
        inputs_x,
        input_b,
        steps,
        a_log,
        dt_bias,
        smem=True,
        hbm=True,
        room=ROOM,
        scratch=[
            pltpu.VMEM(inputs_x.shape, BF16),
            pltpu.VMEM(input_b.shape, BF16),
            pltpu.VMEM(steps.shape, F32),
            pltpu.VMEM(a_log.shape, F32),
            pltpu.VMEM(dt_bias.shape, F32),
            pltpu.SemaphoreType.DMA((5,)),
        ],
    )

    def before():
        return call(
            within_kernel,
            [wide, wide, wide, wide],
            lengths,
            inputs_x,
            gate_z,
            cotangent,
            input_b,
            input_c,
            summed,
            deltas,
            skip_d,
            smem=True,
        )

    entering, marks, (within, fresh, gate, gated) = carry(own, before)
    core, bent, sums = call(
        output_kernel,
        [wide, wide, like((lax.axis_size("tensor"), 2 * rows // LANES, LANES))],
        within,
        fresh,
        gate,
        gated,
        input_c,
        gain,
        entering,
    )
    sums = exchange(sums, "tensor")
    pulled, own_back = call(
        functools.partial(pull_kernel, channels),
        [wide, message],
        core,
        bent,
        gated,
        fresh,
        input_c,
        gain,
        sums,
    )

    def after():
        return call(
            inner_kernel,
            [
                wide,
                wide,
                like((STATE, width)),
                like((rows, STATE)),
                like((rows, STATE), BF16),
                turned,
                turned,
            ],
            lengths,
            inputs_x,
            input_b,
            input_c,
            summed,
            deltas,
            skip_d,
            core,
            pulled,
            fresh,
            entering,
            own,
            smem=True,
        )

    later, gains, beside = carry_back(own_back, marks, after)
    base, weights, leaving, b_part, grad_c, along, back = beside
    share = width // (GROUP * lax.axis_size("zh"))
    grad_x, grad_b, grad_dt, grad_gain = call(
        final_kernel,
        [like((rows, width), BF16), like((rows, STATE), BF16), turned, like((1, share))],
        inputs_x,
        input_b,
        steps,
        a_log,
        dt_bias,
        base,
        weights,
        leaving,
        b_part,
        along,
        back,
        later,
        gains,
    )
    return (grad_x, grad_b, grad_c, grad_dt.T, grad_gain[0])


def solution(mesh):
    count, across = mesh.devices.shape
    split_mesh = Mesh(
        mesh.devices.reshape(count // GROUP, 2, GROUP // 2, across), ("zh", "zl", "x", "tensor")
    )
    tokens = ("zh", "zl", "x")
    both = P(tokens, "tensor")
    alone = P("tensor")
    return jax.shard_map(
        per_device,
        mesh=split_mesh,
        in_specs=(both, both, both, both, both, alone, alone, alone, alone, P(), both),
        out_specs=(both, both, both, both, P(("tensor", "zh", "zl", "x"))),
        check_vma=False,
    )
```

```python
import functools

import jax
import jax.numpy as jnp
from jax import lax
from jax.experimental import pallas as pl
from jax.experimental.pallas import tpu as pltpu
from jax.sharding import Mesh
from jax.sharding import PartitionSpec as P

HEAD_DIM = 64
STATE = 128
STRETCH = 128
LANES = 128
WIDE = 2 * LANES
GROUP = 8
EPSILON = 1e-05
F32 = jnp.float32
BF16 = jnp.bfloat16
NN = (((1,), (0,)), ((), ()))
NT = (((1,), (1,)), ((), ()))


def mul(a, b, dims=NN):
    return lax.dot_general(a, b, dims, preferred_element_type=F32)


def split(a):
    high = a.astype(BF16)
    return (high, (a - high.astype(F32)).astype(BF16))


def mul_sx(a, b, dims=NN):
    return mul(a[0], b, dims) + mul(a[1], b, dims)


def mul_xs(a, b, dims=NN):
    return mul(a, b[0], dims) + mul(a, b[1], dims)


def mul_ss(a, b, dims=NN):
    return mul(a[0], b[0], dims) + (mul(a[0], b[1], dims) + mul(a[1], b[0], dims))


def mul_3x(a, b, dims=NN):
    high = a.astype(BF16)
    rest = a - high.astype(F32)
    middle = rest.astype(BF16)
    low = (rest - middle.astype(F32)).astype(BF16)
    return mul(high, b, dims) + (mul(middle, b, dims) + mul(low, b, dims))


def spread(a, pair):
    rows = a.shape[0]
    lane = lax.broadcasted_iota(jnp.int32, (rows, LANES), 1)
    tiles = []
    for one in (4 * pair, 4 * pair + 2):
        left = jnp.broadcast_to(a[:, one : one + 1], (rows, LANES))
        right = jnp.broadcast_to(a[:, one + 1 : one + 2], (rows, LANES))
        tiles.append(jnp.where(lane < HEAD_DIM, left, right))
    return jnp.concatenate(tiles, axis=1)


def cols(pair):
    return pl.ds(pair * WIDE, WIDE)


def two_tiles(ref, pair, place):
    return jnp.concatenate([ref[2 * pair, place, :], ref[2 * pair + 1, place, :]], axis=1)


def head_marks(heads, pair):
    head = lax.broadcasted_iota(jnp.int32, (heads, WIDE), 0)
    lane = lax.broadcasted_iota(jnp.int32, (heads, WIDE), 1)
    start = (head - 4 * pair) * HEAD_DIM
    return jnp.where((lane >= start) & (lane < start + HEAD_DIM), 1.0, 0.0).astype(BF16)


def ordered(rows):
    at = lax.broadcasted_iota(jnp.int32, (rows, rows), 0)
    of = lax.broadcasted_iota(jnp.int32, (rows, rows), 1)
    return (at, of)


def member_index():
    return lax.axis_index("zl") * lax.axis_size("x") + lax.axis_index("x")


def place_marks(lengths_ref, rows, axis):
    shape = (rows, 1) if axis == 0 else (1, rows)
    docs = lengths_ref.shape[0]
    first = (lax.axis_index("zh") * GROUP + member_index()) * rows
    live_end = rows * GROUP * lax.axis_size("zh") - STRETCH
    places = first + lax.broadcasted_iota(jnp.int32, shape, axis)
    resets = jnp.maximum(places - live_end + 1, 0)
    start = jnp.int32(0)
    for doc in range(docs):
        inside = jnp.where(start >= first, 1, 0)
        resets = resets + jnp.where(places >= start, inside, 0)
        start = start + lengths_ref[doc]
    return (places < live_end, resets)


def softplus(value):
    return jnp.maximum(value, 0.0) + jnp.log1p(jnp.exp(-jnp.abs(value)))


def sigmoid(value):
    return 1.0 / (1.0 + jnp.exp(-value))


def column(row):
    at, of = ordered(row.shape[1])
    return jnp.sum(jnp.where(at == of, row, 0.0), axis=1, keepdims=True)


def states_kernel(
    lengths_hbm,
    x_hbm,
    b_hbm,
    dt_hbm,
    alog_hbm,
    bias_hbm,
    out_ref,
    summed_ref,
    deltas_ref,
    lengths_ref,
    x_ref,
    b_ref,
    dt_ref,
    alog_ref,
    bias_ref,
    sems,
):
    rows = x_ref.shape[0]
    pairs = x_ref.shape[1] // WIDE
    moves = [(alog_hbm, alog_ref), (bias_hbm, bias_ref), (dt_hbm, dt_ref)]
    moves += [(lengths_hbm, lengths_ref), (b_hbm, b_ref), (x_hbm, x_ref)]
    copies = [
        pltpu.make_async_copy(source, target, sems.at[one])
        for one, (source, target) in enumerate(moves)
    ]
    for copy in copies:
        copy.start()
    at, of = ordered(rows)
    before = jnp.where(at <= of, 1.0, 0.0).astype(BF16)
    for copy in copies[:3]:
        copy.wait()
    deltas = softplus(dt_ref[...] + column(bias_ref[...]))
    summed = mul_3x(-jnp.exp(column(alog_ref[...])) * deltas, before)
    ending = summed[:, rows - 1 : rows]
    copies[3].wait()
    _, resets = place_marks(lengths_ref, rows, 1)
    last = resets[:, rows - 1 : rows]
    weights = (jnp.where(resets == last, jnp.exp(ending - summed), 0.0) * deltas).T
    through = jnp.broadcast_to(jnp.where(last == 0, jnp.exp(ending), 0.0), (deltas.shape[0], 8)).T
    copies[4].wait()
    b_turned = b_ref[...].astype(F32).T.astype(BF16)
    copies[5].wait()
    for pair in range(pairs):
        weighted = x_ref[:, cols(pair)].astype(F32) * spread(weights, pair)
        state = mul_xs(b_turned, split(weighted))
        marks = spread(through, pair)
        for half in range(2):
            lanes = slice(half * LANES, (half + 1) * LANES)
            out_ref[2 * pair + half, 0:STATE, :] = state[:, lanes]
            out_ref[2 * pair + half, STATE : STATE + 8, :] = marks[:, lanes]
    summed_ref[...] = summed.T
    deltas_ref[...] = deltas.T


def within_kernel(
    lengths_ref,
    x_ref,
    z_ref,
    cot_ref,
    b_ref,
    c_ref,
    summed_ref,
    deltas_ref,
    skip_ref,
    out_ref,
    fresh_ref,
    gate_ref,
    gated_ref,
):
    rows = x_ref.shape[0]
    pairs = x_ref.shape[1] // WIDE
    living, resets = place_marks(lengths_ref, rows, 0)
    _, resets_row = place_marks(lengths_ref, rows, 1)
    deltas, summed = deltas_ref[...], summed_ref[...]
    middle = summed[rows // 2 - 1 : rows // 2, :]
    rising = jnp.exp(summed - middle)
    falling = jnp.exp(middle - summed) * deltas
    fresh = jnp.where(resets == 0, jnp.exp(summed), 0.0)
    at, of = ordered(rows)
    allowed = (at >= of) & (resets == resets_row)
    crossing = split(jnp.where(allowed, mul(c_ref[...], b_ref[...], NT), 0.0))
    skip = skip_ref[...]
    for pair in range(pairs):
        x = x_ref[:, cols(pair)].astype(F32)
        inner = mul_ss(crossing, split(x * spread(falling, pair)))
        out_ref[:, cols(pair)] = inner * spread(rising, pair) + x * spread(skip, pair)
        fresh_ref[:, cols(pair)] = spread(fresh, pair)
        z = z_ref[:, cols(pair)].astype(F32)
        gate = jnp.where(living, z * sigmoid(z), 0.0)
        gate_ref[:, cols(pair)] = gate
        gated_ref[:, cols(pair)] = gate * cot_ref[:, cols(pair)].astype(F32)


def output_kernel(
    within_ref,
    fresh_ref,
    gate_ref,
    gated_ref,
    c_ref,
    gain_ref,
    entering_ref,
    core_ref,
    bent_ref,
    sums_ref,
):
    rows, width = within_ref.shape
    c = c_ref[...]
    c_twice = jnp.concatenate([c, c], axis=1)
    squares = jnp.zeros((rows, WIDE), F32)
    products = jnp.zeros((rows, WIDE), F32)
    for pair in range(width // WIDE):
        entering = split(two_tiles(entering_ref, pair, slice(None)))
        carried = mul(c_twice, jnp.concatenate(entering, axis=0))
        core = within_ref[:, cols(pair)] + carried * fresh_ref[:, cols(pair)]
        core_ref[:, cols(pair)] = core
        gate = gate_ref[:, cols(pair)]
        shaped = core * gate
        bent_ref[:, cols(pair)] = shaped * gate
        squares += shaped * shaped
        products += gain_ref[:, cols(pair)] * (gated_ref[:, cols(pair)] * core)
    ones = jnp.ones((8, WIDE), BF16)
    for row, total in enumerate((squares, products)):
        high, low = split(total)
        rest = (total - high.astype(F32) - low.astype(F32)).astype(BF16)
        sum_row = mul(ones, high, NT) + (mul(ones, low, NT) + mul(ones, rest, NT))
        for half in range(2):
            line = 2 * row + half
            for to in range(sums_ref.shape[0]):
                sums_ref[to, line : line + 1, :] = sum_row[0:1, half * LANES : (half + 1) * LANES]


def pull_kernel(
    channels,
    core_ref,
    bent_ref,
    gated_ref,
    fresh_ref,
    c_ref,
    gain_ref,
    sums_ref,
    pull_ref,
    out_ref,
):
    rows, width = core_ref.shape
    sums = sums_ref[0]
    for other in range(1, sums_ref.shape[0]):
        sums = sums + sums_ref[other]
    squares = jnp.concatenate([sums[0:1], sums[1:2]], axis=1)
    products = jnp.concatenate([sums[2:3], sums[3:4]], axis=1)
    scaling_row = lax.rsqrt(squares / channels + EPSILON)
    second_row = scaling_row * scaling_row * scaling_row * products / channels
    scaling = column(scaling_row)
    second = column(second_row)
    c_turned = c_ref[...].astype(F32).T.astype(BF16)
    gains = []
    for pair in range(width // WIDE):
        scaled = gated_ref[:, cols(pair)] * scaling
        gain_sum = jnp.sum(scaled * core_ref[:, cols(pair)], axis=0, keepdims=True)
        gains += [gain_sum[:, :LANES], gain_sum[:, LANES:]]
        pulled = scaled * gain_ref[:, cols(pair)] - second * bent_ref[:, cols(pair)]
        pull_ref[:, cols(pair)] = pulled
        state = mul_xs(c_turned, split(pulled * fresh_ref[:, cols(pair)]))
        out_ref[2 * pair, 0:STATE, :] = state[:, :LANES]
        out_ref[2 * pair + 1, 0:STATE, :] = state[:, LANES:]
    for member in range(GROUP):
        for one in range(GROUP):
            out_ref[member, STATE + one : STATE + one + 1, :] = gains[one]


def inner_kernel(
    lengths_ref,
    x_ref,
    b_ref,
    c_ref,
    summed_ref,
    deltas_ref,
    skip_ref,
    core_ref,
    pull_ref,
    fresh_ref,
    entering_ref,
    own_ref,
    base_ref,
    weights_ref,
    high_ref,
    low_ref,
    leaving_ref,
    b_out_ref,
    c_out_ref,
    along_ref,
    back_ref,
):
    rows = x_ref.shape[0]
    pairs = x_ref.shape[1] // WIDE
    _, resets = place_marks(lengths_ref, rows, 0)
    _, resets_row = place_marks(lengths_ref, rows, 1)
    deltas, summed = deltas_ref[...], summed_ref[...]
    heads = deltas.shape[1]
    middle = summed[rows // 2 - 1 : rows // 2, :]
    rising = jnp.exp(summed - middle)
    falling = jnp.exp(middle - summed) * deltas
    ending = summed[rows - 1 : rows, :]
    last = resets[rows - 1 : rows, :]
    weights = jnp.where(resets == last, jnp.exp(ending - summed), 0.0) * deltas
    at, of = ordered(rows)
    same = resets == resets_row
    b, c = b_ref[...], c_ref[...]
    turned = split(jnp.where((at <= of) & same, mul(b, c, NT), 0.0))
    skip = skip_ref[...]
    paired = jnp.zeros((rows, rows), F32)
    c_sum = jnp.zeros((rows, STATE), F32)
    along = jnp.zeros((heads, rows), F32)
    back = jnp.zeros((heads, rows), F32)
    for pair in range(pairs):
        pulled = pull_ref[:, cols(pair)]
        x = x_ref[:, cols(pair)].astype(F32)
        raised = split(pulled * spread(rising, pair))
        lowered = spread(falling, pair)
        direct = mul_ss(turned, raised) * lowered
        skipped = spread(skip, pair)
        base_ref[:, cols(pair)] = direct + skipped * pulled
        spread_weights = spread(weights, pair)
        weights_ref[:, cols(pair)] = spread_weights
        high_ref[:, cols(pair)], low_ref[:, cols(pair)] = split(x * spread_weights)
        paired += mul_ss(raised, split(x * lowered), NT)
        entering = two_tiles(entering_ref, pair, slice(None))
        c_sum += mul_ss(split(pulled * fresh_ref[:, cols(pair)]), split(entering), NT)
        marks = head_marks(heads, pair)
        along += mul_xs(marks, split(pulled * (core_ref[:, cols(pair)] - x * skipped)), NT)
        back += mul_xs(marks, split(x * direct), NT)
        through = two_tiles(own_ref, pair, slice(STATE, STATE + 1))
        leaving = through * entering + two_tiles(own_ref, pair, slice(0, STATE))
        leaving_ref[:, cols(pair)] = leaving
    paired = jnp.where((at >= of) & same, paired, 0.0)
    c_out_ref[...] = (c_sum + mul_sx(split(paired), b)).astype(BF16)
    b_out_ref[...] = mul_sx(split(paired.T), c)
    along_ref[...] = along
    back_ref[...] = back


def final_kernel(
    x_ref,
    b_ref,
    dt_ref,
    alog_ref,
    bias_ref,
    base_ref,
    weights_ref,
    high_ref,
    low_ref,
    leaving_ref,
    b_in_ref,
    along_ref,
    back_ref,
    later_ref,
    gains_ref,
    x_out_ref,
    b_out_ref,
    dt_out_ref,
    gain_out_ref,
):
    rows = x_ref.shape[0]
    heads = dt_ref.shape[0]
    table = gains_ref[0]
    for one in range(1, gains_ref.shape[0]):
        table = table + gains_ref[one]
    table = jnp.broadcast_to(table, (8, LANES))
    share = gain_out_ref.shape[1]
    lane = lax.broadcasted_iota(jnp.int32, (LANES, share), 0)
    place = lax.broadcasted_iota(jnp.int32, (LANES, share), 1)
    chosen = jnp.where(lane == place + share * member_index(), 1.0, 0.0).astype(BF16)
    gain_out_ref[...] = mul_3x(table, chosen)[0:1]
    b = b_ref[...]
    b_twice = jnp.concatenate([b, b], axis=1)
    b_sum = b_in_ref[...]
    back = back_ref[...]
    ends = jnp.zeros((heads, 8), F32)
    for pair in range(x_ref.shape[1] // WIDE):
        later_full = two_tiles(later_ref, pair, slice(None))
        later = split(later_full)
        weights = weights_ref[:, cols(pair)]
        gained = mul(b_twice, jnp.concatenate(later, axis=0)) * weights
        x_out_ref[:, cols(pair)] = (base_ref[:, cols(pair)] + gained).astype(BF16)
        x = x_ref[:, cols(pair)].astype(F32)
        both = mul(high_ref[:, cols(pair)], jnp.concatenate(later, axis=0), NT)
        b_sum += both[:, :STATE] + (both[:, STATE:] + mul(low_ref[:, cols(pair)], later[0], NT))
        marks = head_marks(heads, pair)
        back += mul_xs(marks, split(x * gained), NT)
        end = jnp.sum(later_full * leaving_ref[:, cols(pair)], axis=0, keepdims=True)
        ends += mul_xs(marks, split(jnp.broadcast_to(end, (8, WIDE))), NT)
    b_out_ref[...] = b_sum.astype(BF16)
    at, of = ordered(rows)
    after = jnp.where(at >= of, 1.0, 0.0).astype(BF16)
    log_pull = mul_3x(along_ref[...] - back, after) + ends[:, 0:1]
    raw = dt_ref[...] + column(bias_ref[...])
    direct = back / softplus(raw)
    dt_out_ref[...] = (direct - jnp.exp(column(alog_ref[...])) * log_pull) * sigmoid(raw)


def gather_kernel(reverse, got_ref, marks_ref, out_ref, *gain_ref):
    order = list(range(GROUP))
    if reverse:
        order.reverse()
    joined = got_ref[order[0], 0:STATE, :]
    marks = marks_ref[0, STATE : STATE + 8, :]
    for one in order[1:]:
        joined = marks_ref[one, STATE : STATE + 1, :] * joined + got_ref[one, 0:STATE, :]
    for one in range(1, GROUP):
        marks = marks * marks_ref[one, STATE : STATE + 8, :]
    end = out_ref.shape[0] - 8
    out_ref[0:STATE, :] = joined
    out_ref[end : end + 8, :] = marks
    if reverse:
        gain = got_ref[0, STATE : STATE + 8, :]
        for one in range(1, GROUP):
            gain = gain + got_ref[one, STATE : STATE + 8, :]
        gain_ref[0][...] = gain


def join_kernel(own_ref, got_ref, out_ref, far_ref):
    through = own_ref[STATE : STATE + 1, :]
    joined = own_ref[0:STATE, :] + through * got_ref[0:STATE, :]
    out_ref[0:STATE, :] = joined
    far_ref[0:STATE, :] = joined
    out_ref[STATE : STATE + 8, :] = own_ref[STATE : STATE + 8, :] * got_ref[STATE : STATE + 8, :]


def hand_members(holding, reverse, got_ref, marks_ref, out_ref):
    order = list(range(GROUP))
    if reverse:
        order.reverse()
    for one in order:
        out_ref[one] = holding
        if one != order[-1]:
            through = marks_ref[one, STATE : STATE + 1, :]
            holding = through * holding + got_ref[one, 0:STATE, :]


def hand_kernel(reverse, near_ref, far_ref, got_ref, marks_ref, out_ref):
    through = near_ref[STATE : STATE + 1, :]
    holding = near_ref[0:STATE, :] + through * far_ref[0:STATE, :]
    hand_members(holding, reverse, got_ref, marks_ref, out_ref)


def call(kernel, outs, *operands, smem=False, hbm=False, scratch=()):
    space = pltpu.HBM if hbm else pltpu.VMEM
    in_specs = [jax.tree.map(lambda _: pl.BlockSpec(memory_space=space), one) for one in operands]
    if smem:
        in_specs[0] = pl.BlockSpec(memory_space=pltpu.SMEM)
    if hbm:
        operands = [pltpu.with_memory_space_constraint(one, pltpu.HBM) for one in operands]
    many = isinstance(outs, (list, tuple))
    spec = pl.BlockSpec(memory_space=pltpu.VMEM)
    return pl.pallas_call(
        kernel,
        out_shape=outs,
        in_specs=in_specs,
        out_specs=[spec] * len(outs) if many else spec,
        scratch_shapes=scratch,
        compiler_params=pltpu.CompilerParams(vmem_limit_bytes=16 * 1024 * 1024),
    )(*operands)


def like(shape, kind=F32):
    return jax.ShapeDtypeStruct(shape, kind)


def exchange(value, axes):
    return lax.all_to_all(value, axes, 0, 0, tiled=True)


def moved(value, by, around):
    count = lax.axis_size("zh")
    pairs = [(i, i + by) for i in range(count)]
    if around:
        pairs = [(i, j % count) for i, j in pairs]
    return lax.ppermute(value, "zh", [(i, j) for i, j in pairs if 0 <= j < count])


def carry(own, beside):
    got = exchange(own, ("zl", "x"))
    message, tile = like(own.shape[1:]), like((STATE, LANES))
    joined = call(functools.partial(gather_kernel, False), message, got, got)
    from_next = moved(joined, 1, False)
    from_next, beside = lax.optimization_barrier((from_next, beside()))
    twice, state = call(join_kernel, [message, tile], joined, from_next)
    handed = call(
        functools.partial(hand_kernel, False),
        like((GROUP, STATE, LANES)),
        moved(twice, 1, False),
        moved(state, 3, False),
        got,
        got,
    )
    return (exchange(handed, ("zl", "x")), got, beside)


def carry_back(own, marks, beside):
    got = exchange(own, ("zl", "x"))
    message, table, tile = like((STATE + 8, LANES)), like((8, LANES)), like((STATE, LANES))
    joined, gain = call(functools.partial(gather_kernel, True), [message, table], got, marks)
    gains = exchange(gain[:, None, :], "zh")
    from_next, beside = lax.optimization_barrier((moved(joined, -1, False), beside()))
    twice, state = call(join_kernel, [message, tile], joined, from_next)
    near, far = moved(twice, -1, False), moved(state, -3, False)
    near, far, gains = lax.optimization_barrier((near, far, gains))
    handed = call(
        functools.partial(hand_kernel, True),
        like((GROUP, STATE, LANES)),
        near,
        far,
        got,
        marks,
    )
    return (exchange(handed, ("zl", "x")), gains, beside)


def per_device(
    inputs_x,
    gate_z,
    input_b,
    input_c,
    dt_raw,
    a_log,
    dt_bias,
    skip_d,
    norm_gain,
    lengths,
    cotangent,
):
    rows, width = inputs_x.shape
    heads = dt_raw.shape[1]
    channels = float(width * lax.axis_size("tensor"))
    steps = dt_raw.T
    a_log, dt_bias = a_log[None, :], dt_bias[None, :]
    skip_d, gain = skip_d[None, :], norm_gain[None, :]
    message = like((GROUP, STATE + 8, LANES))
    wide = like((rows, width))
    small = like((rows, heads))
    turned = like((heads, rows))

    own, summed, deltas = call(
        states_kernel,
        [message, small, small],
        lengths,
        inputs_x,
        input_b,
        steps,
        a_log,
        dt_bias,
        hbm=True,
        scratch=[
            pltpu.SMEM(lengths.shape, jnp.int32),
            pltpu.VMEM(inputs_x.shape, BF16),
            pltpu.VMEM(input_b.shape, BF16),
            pltpu.VMEM(steps.shape, F32),
            pltpu.VMEM(a_log.shape, F32),
            pltpu.VMEM(dt_bias.shape, F32),
            pltpu.SemaphoreType.DMA((6,)),
        ],
    )

    def before():
        return call(
            within_kernel,
            [wide, wide, wide, wide],
            lengths,
            inputs_x,
            gate_z,
            cotangent,
            input_b,
            input_c,
            summed,
            deltas,
            skip_d,
            smem=True,
        )

    entering, marks, (within, fresh, gate, gated) = carry(own, before)
    core, bent, sums = call(
        output_kernel,
        [wide, wide, like((lax.axis_size("tensor"), 2 * rows // LANES, LANES))],
        within,
        fresh,
        gate,
        gated,
        input_c,
        gain,
        entering,
    )
    sums = exchange(sums, "tensor")
    pulled, own_back = call(
        functools.partial(pull_kernel, channels),
        [wide, message],
        core,
        bent,
        gated,
        fresh,
        input_c,
        gain,
        sums,
    )

    def after():
        return call(
            inner_kernel,
            [
                wide,
                wide,
                like((rows, width), BF16),
                like((rows, width), BF16),
                like((STATE, width)),
                like((rows, STATE)),
                like((rows, STATE), BF16),
                turned,
                turned,
            ],
            lengths,
            inputs_x,
            input_b,
            input_c,
            summed,
            deltas,
            skip_d,
            core,
            pulled,
            fresh,
            entering,
            own,
            smem=True,
        )

    later, gains, beside = carry_back(own_back, marks, after)
    base, weights, high, low, leaving, b_part, grad_c, along, back = beside
    share = width // (GROUP * lax.axis_size("zh"))
    grad_x, grad_b, grad_dt, grad_gain = call(
        final_kernel,
        [like((rows, width), BF16), like((rows, STATE), BF16), turned, like((1, share))],
        inputs_x,
        input_b,
        steps,
        a_log,
        dt_bias,
        base,
        weights,
        high,
        low,
        leaving,
        b_part,
        along,
        back,
        later,
        gains,
    )
    return (grad_x, grad_b, grad_c, grad_dt.T, grad_gain[0])


def solution(mesh):
    count, across = mesh.devices.shape
    split_mesh = Mesh(
        mesh.devices.reshape(count // GROUP, 2, GROUP // 2, across), ("zh", "zl", "x", "tensor")
    )
    tokens = ("zh", "zl", "x")
    both = P(tokens, "tensor")
    alone = P("tensor")
    return jax.shard_map(
        per_device,
        mesh=split_mesh,
        in_specs=(both, both, both, both, both, alone, alone, alone, alone, P(), both),
        out_specs=(both, both, both, both, P(("tensor", "zh", "zl", "x"))),
        check_vma=False,
    )
```

```python
import functools

import jax
import jax.numpy as jnp
from jax import lax
from jax.experimental import pallas as pl
from jax.experimental.pallas import tpu as pltpu
from jax.sharding import Mesh
from jax.sharding import PartitionSpec as P

HEAD_DIM = 64
STATE = 128
STRETCH = 128
LANES = 128
WIDE = 2 * LANES
GROUP = 8
EPSILON = 1e-05
F32 = jnp.float32
BF16 = jnp.bfloat16
NN = (((1,), (0,)), ((), ()))
NT = (((1,), (1,)), ((), ()))


def mul(a, b, dims=NN):
    return lax.dot_general(a, b, dims, preferred_element_type=F32)


def split(a):
    high = a.astype(BF16)
    return (high, (a - high.astype(F32)).astype(BF16))


def mul_sx(a, b, dims=NN):
    return mul(a[0], b, dims) + mul(a[1], b, dims)


def mul_xs(a, b, dims=NN):
    return mul(a, b[0], dims) + mul(a, b[1], dims)


def mul_ss(a, b, dims=NN):
    return mul(a[0], b[0], dims) + (mul(a[0], b[1], dims) + mul(a[1], b[0], dims))


def mul_3x(a, b, dims=NN):
    high = a.astype(BF16)
    rest = a - high.astype(F32)
    middle = rest.astype(BF16)
    low = (rest - middle.astype(F32)).astype(BF16)
    return mul(high, b, dims) + (mul(middle, b, dims) + mul(low, b, dims))


def spread(a, pair):
    rows = a.shape[0]
    lane = lax.broadcasted_iota(jnp.int32, (rows, LANES), 1)
    tiles = []
    for one in (4 * pair, 4 * pair + 2):
        left = jnp.broadcast_to(a[:, one : one + 1], (rows, LANES))
        right = jnp.broadcast_to(a[:, one + 1 : one + 2], (rows, LANES))
        tiles.append(jnp.where(lane < HEAD_DIM, left, right))
    return jnp.concatenate(tiles, axis=1)


def cols(pair):
    return pl.ds(pair * WIDE, WIDE)


def two_tiles(ref, pair, place):
    return jnp.concatenate([ref[2 * pair, place, :], ref[2 * pair + 1, place, :]], axis=1)


def head_marks(heads, pair):
    head = lax.broadcasted_iota(jnp.int32, (heads, WIDE), 0)
    lane = lax.broadcasted_iota(jnp.int32, (heads, WIDE), 1)
    start = (head - 4 * pair) * HEAD_DIM
    return jnp.where((lane >= start) & (lane < start + HEAD_DIM), 1.0, 0.0).astype(BF16)


def ordered(rows):
    at = lax.broadcasted_iota(jnp.int32, (rows, rows), 0)
    of = lax.broadcasted_iota(jnp.int32, (rows, rows), 1)
    return (at, of)


def member_index():
    return lax.axis_index("zl") * lax.axis_size("x") + lax.axis_index("x")


def place_marks(lengths_ref, rows, axis):
    shape = (rows, 1) if axis == 0 else (1, rows)
    docs = lengths_ref.shape[0]
    first = (lax.axis_index("zh") * GROUP + member_index()) * rows
    live_end = rows * GROUP * lax.axis_size("zh") - STRETCH
    places = first + lax.broadcasted_iota(jnp.int32, shape, axis)
    resets = jnp.maximum(places - live_end + 1, 0)
    start = jnp.int32(0)
    for doc in range(docs):
        inside = jnp.where(start >= first, 1, 0)
        resets = resets + jnp.where(places >= start, inside, 0)
        start = start + lengths_ref[doc]
    return (places < live_end, resets)


def softplus(value):
    return jnp.maximum(value, 0.0) + jnp.log1p(jnp.exp(-jnp.abs(value)))


def sigmoid(value):
    return 1.0 / (1.0 + jnp.exp(-value))


def column(row):
    at, of = ordered(row.shape[1])
    return jnp.sum(jnp.where(at == of, row, 0.0), axis=1, keepdims=True)


def states_kernel(
    lengths_hbm,
    x_hbm,
    b_hbm,
    dt_hbm,
    alog_hbm,
    bias_hbm,
    out_ref,
    summed_ref,
    deltas_ref,
    lengths_ref,
    x_ref,
    b_ref,
    dt_ref,
    alog_ref,
    bias_ref,
    sems,
):
    rows = x_ref.shape[0]
    pairs = x_ref.shape[1] // WIDE
    moves = [(alog_hbm, alog_ref), (bias_hbm, bias_ref), (dt_hbm, dt_ref)]
    moves += [(lengths_hbm, lengths_ref), (b_hbm, b_ref), (x_hbm, x_ref)]
    copies = [
        pltpu.make_async_copy(source, target, sems.at[one])
        for one, (source, target) in enumerate(moves)
    ]
    for copy in copies:
        copy.start()
    at, of = ordered(rows)
    before = jnp.where(at <= of, 1.0, 0.0).astype(BF16)
    for copy in copies[:3]:
        copy.wait()
    deltas = softplus(dt_ref[...] + column(bias_ref[...]))
    summed = mul_3x(-jnp.exp(column(alog_ref[...])) * deltas, before)
    ending = summed[:, rows - 1 : rows]
    copies[3].wait()
    _, resets = place_marks(lengths_ref, rows, 1)
    last = resets[:, rows - 1 : rows]
    weights = (jnp.where(resets == last, jnp.exp(ending - summed), 0.0) * deltas).T
    through = jnp.broadcast_to(jnp.where(last == 0, jnp.exp(ending), 0.0), (deltas.shape[0], 8)).T
    copies[4].wait()
    b_turned = b_ref[...].astype(F32).T.astype(BF16)
    copies[5].wait()
    for pair in range(pairs):
        weighted = x_ref[:, cols(pair)].astype(F32) * spread(weights, pair)
        state = mul_xs(b_turned, split(weighted))
        marks = spread(through, pair)
        for half in range(2):
            lanes = slice(half * LANES, (half + 1) * LANES)
            out_ref[2 * pair + half, 0:STATE, :] = state[:, lanes]
            out_ref[2 * pair + half, STATE : STATE + 8, :] = marks[:, lanes]
    summed_ref[...] = summed.T
    deltas_ref[...] = deltas.T


def within_kernel(
    lengths_ref,
    x_ref,
    z_ref,
    cot_ref,
    b_ref,
    c_ref,
    summed_ref,
    deltas_ref,
    skip_ref,
    out_ref,
    fresh_ref,
    gate_ref,
    gated_ref,
):
    rows = x_ref.shape[0]
    pairs = x_ref.shape[1] // WIDE
    living, resets = place_marks(lengths_ref, rows, 0)
    _, resets_row = place_marks(lengths_ref, rows, 1)
    deltas, summed = deltas_ref[...], summed_ref[...]
    middle = summed[rows // 2 - 1 : rows // 2, :]
    rising = jnp.exp(summed - middle)
    falling = jnp.exp(middle - summed) * deltas
    fresh = jnp.where(resets == 0, jnp.exp(summed), 0.0)
    at, of = ordered(rows)
    allowed = (at >= of) & (resets == resets_row)
    crossing = split(jnp.where(allowed, mul(c_ref[...], b_ref[...], NT), 0.0))
    skip = skip_ref[...]
    for pair in range(pairs):
        x = x_ref[:, cols(pair)].astype(F32)
        inner = mul_ss(crossing, split(x * spread(falling, pair)))
        out_ref[:, cols(pair)] = inner * spread(rising, pair) + x * spread(skip, pair)
        fresh_ref[:, cols(pair)] = spread(fresh, pair)
        z = z_ref[:, cols(pair)].astype(F32)
        gate = jnp.where(living, z * sigmoid(z), 0.0)
        gate_ref[:, cols(pair)] = gate
        gated_ref[:, cols(pair)] = gate * cot_ref[:, cols(pair)].astype(F32)


def output_kernel(
    within_ref,
    fresh_ref,
    gate_ref,
    gated_ref,
    c_ref,
    gain_ref,
    entering_ref,
    core_ref,
    bent_ref,
    sums_ref,
):
    rows, width = within_ref.shape
    c = c_ref[...]
    c_twice = jnp.concatenate([c, c], axis=1)
    squares = jnp.zeros((rows, WIDE), F32)
    products = jnp.zeros((rows, WIDE), F32)
    for pair in range(width // WIDE):
        entering = split(two_tiles(entering_ref, pair, slice(None)))
        carried = mul(c_twice, jnp.concatenate(entering, axis=0))
        core = within_ref[:, cols(pair)] + carried * fresh_ref[:, cols(pair)]
        core_ref[:, cols(pair)] = core
        gate = gate_ref[:, cols(pair)]
        shaped = core * gate
        bent_ref[:, cols(pair)] = shaped * gate
        squares += shaped * shaped
        products += gain_ref[:, cols(pair)] * (gated_ref[:, cols(pair)] * core)
    ones = jnp.ones((8, WIDE), BF16)
    for row, total in enumerate((squares, products)):
        high, low = split(total)
        rest = (total - high.astype(F32) - low.astype(F32)).astype(BF16)
        sum_row = mul(ones, high, NT) + (mul(ones, low, NT) + mul(ones, rest, NT))
        for half in range(2):
            line = 2 * row + half
            for to in range(sums_ref.shape[0]):
                sums_ref[to, line : line + 1, :] = sum_row[0:1, half * LANES : (half + 1) * LANES]


def pull_kernel(
    channels,
    core_ref,
    bent_ref,
    gated_ref,
    fresh_ref,
    c_ref,
    gain_ref,
    sums_ref,
    pull_ref,
    out_ref,
):
    rows, width = core_ref.shape
    sums = sums_ref[0]
    for other in range(1, sums_ref.shape[0]):
        sums = sums + sums_ref[other]
    squares = jnp.concatenate([sums[0:1], sums[1:2]], axis=1)
    products = jnp.concatenate([sums[2:3], sums[3:4]], axis=1)
    scaling_row = lax.rsqrt(squares / channels + EPSILON)
    second_row = scaling_row * scaling_row * scaling_row * products / channels
    scaling = column(scaling_row)
    second = column(second_row)
    c_turned = c_ref[...].astype(F32).T.astype(BF16)
    gains = []
    for pair in range(width // WIDE):
        scaled = gated_ref[:, cols(pair)] * scaling
        gain_sum = jnp.sum(scaled * core_ref[:, cols(pair)], axis=0, keepdims=True)
        gains += [gain_sum[:, :LANES], gain_sum[:, LANES:]]
        pulled = scaled * gain_ref[:, cols(pair)] - second * bent_ref[:, cols(pair)]
        pull_ref[:, cols(pair)] = pulled
        state = mul_xs(c_turned, split(pulled * fresh_ref[:, cols(pair)]))
        out_ref[2 * pair, 0:STATE, :] = state[:, :LANES]
        out_ref[2 * pair + 1, 0:STATE, :] = state[:, LANES:]
    for member in range(GROUP):
        for one in range(GROUP):
            out_ref[member, STATE + one : STATE + one + 1, :] = gains[one]


def inner_kernel(
    lengths_ref,
    x_ref,
    b_ref,
    c_ref,
    summed_ref,
    deltas_ref,
    skip_ref,
    core_ref,
    pull_ref,
    fresh_ref,
    entering_ref,
    own_ref,
    base_ref,
    weights_ref,
    high_ref,
    low_ref,
    leaving_ref,
    b_out_ref,
    c_out_ref,
    along_ref,
    back_ref,
):
    rows = x_ref.shape[0]
    pairs = x_ref.shape[1] // WIDE
    _, resets = place_marks(lengths_ref, rows, 0)
    _, resets_row = place_marks(lengths_ref, rows, 1)
    deltas, summed = deltas_ref[...], summed_ref[...]
    heads = deltas.shape[1]
    middle = summed[rows // 2 - 1 : rows // 2, :]
    rising = jnp.exp(summed - middle)
    falling = jnp.exp(middle - summed) * deltas
    ending = summed[rows - 1 : rows, :]
    last = resets[rows - 1 : rows, :]
    weights = jnp.where(resets == last, jnp.exp(ending - summed), 0.0) * deltas
    at, of = ordered(rows)
    same = resets == resets_row
    b, c = b_ref[...], c_ref[...]
    turned = split(jnp.where((at <= of) & same, mul(b, c, NT), 0.0))
    skip = skip_ref[...]
    paired = jnp.zeros((rows, rows), F32)
    c_sum = jnp.zeros((rows, STATE), F32)
    along = jnp.zeros((heads, rows), F32)
    back = jnp.zeros((heads, rows), F32)
    for pair in range(pairs):
        pulled = pull_ref[:, cols(pair)]
        x = x_ref[:, cols(pair)].astype(F32)
        raised = split(pulled * spread(rising, pair))
        lowered = spread(falling, pair)
        direct = mul_ss(turned, raised) * lowered
        skipped = spread(skip, pair)
        base_ref[:, cols(pair)] = direct + skipped * pulled
        spread_weights = spread(weights, pair)
        weights_ref[:, cols(pair)] = spread_weights
        high_ref[:, cols(pair)], low_ref[:, cols(pair)] = split(x * spread_weights)
        paired += mul_ss(raised, split(x * lowered), NT)
        entering = two_tiles(entering_ref, pair, slice(None))
        c_sum += mul_ss(split(pulled * fresh_ref[:, cols(pair)]), split(entering), NT)
        marks = head_marks(heads, pair)
        along += mul_xs(marks, split(pulled * (core_ref[:, cols(pair)] - x * skipped)), NT)
        back += mul_xs(marks, split(x * direct), NT)
        through = two_tiles(own_ref, pair, slice(STATE, STATE + 1))
        leaving = through * entering + two_tiles(own_ref, pair, slice(0, STATE))
        leaving_ref[:, cols(pair)] = leaving
    paired = jnp.where((at >= of) & same, paired, 0.0)
    c_out_ref[...] = (c_sum + mul_sx(split(paired), b)).astype(BF16)
    b_out_ref[...] = mul_sx(split(paired.T), c)
    along_ref[...] = along
    back_ref[...] = back


def final_kernel(
    x_ref,
    b_ref,
    dt_ref,
    alog_ref,
    bias_ref,
    base_ref,
    weights_ref,
    high_ref,
    low_ref,
    leaving_ref,
    b_in_ref,
    along_ref,
    back_ref,
    later_ref,
    gains_ref,
    x_out_ref,
    b_out_ref,
    dt_out_ref,
    gain_out_ref,
):
    rows = x_ref.shape[0]
    heads = dt_ref.shape[0]
    table = gains_ref[0]
    for one in range(1, gains_ref.shape[0]):
        table = table + gains_ref[one]
    table = jnp.broadcast_to(table, (8, LANES))
    share = gain_out_ref.shape[1]
    lane = lax.broadcasted_iota(jnp.int32, (LANES, share), 0)
    place = lax.broadcasted_iota(jnp.int32, (LANES, share), 1)
    chosen = jnp.where(lane == place + share * member_index(), 1.0, 0.0).astype(BF16)
    gain_out_ref[...] = mul_3x(table, chosen)[0:1]
    b = b_ref[...]
    b_twice = jnp.concatenate([b, b], axis=1)
    b_sum = b_in_ref[...]
    back = back_ref[...]
    ends = jnp.zeros((heads, 8), F32)
    for pair in range(x_ref.shape[1] // WIDE):
        later_full = two_tiles(later_ref, pair, slice(None))
        later = split(later_full)
        weights = weights_ref[:, cols(pair)]
        gained = mul(b_twice, jnp.concatenate(later, axis=0)) * weights
        x_out_ref[:, cols(pair)] = (base_ref[:, cols(pair)] + gained).astype(BF16)
        x = x_ref[:, cols(pair)].astype(F32)
        both = mul(high_ref[:, cols(pair)], jnp.concatenate(later, axis=0), NT)
        b_sum += both[:, :STATE] + (both[:, STATE:] + mul(low_ref[:, cols(pair)], later[0], NT))
        marks = head_marks(heads, pair)
        back += mul_xs(marks, split(x * gained), NT)
        end = jnp.sum(later_full * leaving_ref[:, cols(pair)], axis=0, keepdims=True)
        ends += mul_xs(marks, split(jnp.broadcast_to(end, (8, WIDE))), NT)
    b_out_ref[...] = b_sum.astype(BF16)
    at, of = ordered(rows)
    after = jnp.where(at >= of, 1.0, 0.0).astype(BF16)
    log_pull = mul_3x(along_ref[...] - back, after) + ends[:, 0:1]
    raw = dt_ref[...] + column(bias_ref[...])
    direct = back / softplus(raw)
    dt_out_ref[...] = (direct - jnp.exp(column(alog_ref[...])) * log_pull) * sigmoid(raw)


def gather_kernel(reverse, got_ref, marks_ref, out_ref, *gain_ref):
    order = list(range(GROUP))
    if reverse:
        order.reverse()
    joined = got_ref[order[0], 0:STATE, :]
    marks = marks_ref[0, STATE : STATE + 8, :]
    for one in order[1:]:
        joined = marks_ref[one, STATE : STATE + 1, :] * joined + got_ref[one, 0:STATE, :]
    for one in range(1, GROUP):
        marks = marks * marks_ref[one, STATE : STATE + 8, :]
    end = out_ref.shape[0] - 8
    out_ref[0:STATE, :] = joined
    out_ref[end : end + 8, :] = marks
    if reverse:
        gain = got_ref[0, STATE : STATE + 8, :]
        for one in range(1, GROUP):
            gain = gain + got_ref[one, STATE : STATE + 8, :]
        gain_ref[0][...] = gain


def join_kernel(own_ref, got_ref, out_ref, far_ref):
    through = own_ref[STATE : STATE + 1, :]
    joined = own_ref[0:STATE, :] + through * got_ref[0:STATE, :]
    out_ref[0:STATE, :] = joined
    far_ref[0:STATE, :] = joined
    out_ref[STATE : STATE + 8, :] = own_ref[STATE : STATE + 8, :] * got_ref[STATE : STATE + 8, :]


def hand_members(holding, reverse, got_ref, marks_ref, out_ref):
    order = list(range(GROUP))
    if reverse:
        order.reverse()
    for one in order:
        out_ref[one] = holding
        if one != order[-1]:
            through = marks_ref[one, STATE : STATE + 1, :]
            holding = through * holding + got_ref[one, 0:STATE, :]


def hand_kernel(reverse, near_ref, far_ref, got_ref, marks_ref, out_ref):
    through = near_ref[STATE : STATE + 1, :]
    holding = near_ref[0:STATE, :] + through * far_ref[0:STATE, :]
    hand_members(holding, reverse, got_ref, marks_ref, out_ref)


def call(kernel, outs, *operands, smem=False, hbm=False, scratch=()):
    space = pltpu.HBM if hbm else pltpu.VMEM
    in_specs = [jax.tree.map(lambda _: pl.BlockSpec(memory_space=space), one) for one in operands]
    if smem:
        in_specs[0] = pl.BlockSpec(memory_space=pltpu.SMEM)
    if hbm:
        operands = [pltpu.with_memory_space_constraint(one, pltpu.HBM) for one in operands]
    many = isinstance(outs, (list, tuple))
    spec = pl.BlockSpec(memory_space=pltpu.VMEM)
    return pl.pallas_call(
        kernel,
        out_shape=outs,
        in_specs=in_specs,
        out_specs=[spec] * len(outs) if many else spec,
        scratch_shapes=scratch,
        compiler_params=pltpu.CompilerParams(vmem_limit_bytes=16 * 1024 * 1024),
    )(*operands)


def like(shape, kind=F32):
    return jax.ShapeDtypeStruct(shape, kind)


def exchange(value, axes):
    return lax.all_to_all(value, axes, 0, 0, tiled=True)


def moved(value, by, around):
    count = lax.axis_size("zh")
    pairs = [(i, i + by) for i in range(count)]
    if around:
        pairs = [(i, j % count) for i, j in pairs]
    return lax.ppermute(value, "zh", [(i, j) for i, j in pairs if 0 <= j < count])


def carry(own, beside):
    got = exchange(own, ("zl", "x"))
    message, tile = like(own.shape[1:]), like((STATE, LANES))
    joined = call(functools.partial(gather_kernel, False), message, got, got)
    from_next = moved(joined, 1, False)
    from_next, beside = lax.optimization_barrier((from_next, beside()))
    twice, state = call(join_kernel, [message, tile], joined, from_next)
    handed = call(
        functools.partial(hand_kernel, False),
        like((GROUP, STATE, LANES)),
        moved(twice, 1, False),
        moved(state, 3, False),
        got,
        got,
    )
    return (exchange(handed, ("zl", "x")), got, beside)


def carry_back(own, marks, beside):
    got = exchange(own, ("zl", "x"))
    message, table, tile = like((STATE + 8, LANES)), like((8, LANES)), like((STATE, LANES))
    joined, gain = call(functools.partial(gather_kernel, True), [message, table], got, marks)
    gains = exchange(gain[:, None, :], "zh")
    from_next, beside = lax.optimization_barrier((moved(joined, -1, False), beside()))
    twice, state = call(join_kernel, [message, tile], joined, from_next)
    near, far = moved(twice, -1, False), moved(state, -3, False)
    near, far, gains = lax.optimization_barrier((near, far, gains))
    handed = call(
        functools.partial(hand_kernel, True),
        like((GROUP, STATE, LANES)),
        near,
        far,
        got,
        marks,
    )
    return (exchange(handed, ("zl", "x")), gains, beside)


def per_device(
    inputs_x,
    gate_z,
    input_b,
    input_c,
    dt_raw,
    a_log,
    dt_bias,
    skip_d,
    norm_gain,
    lengths,
    cotangent,
):
    rows, width = inputs_x.shape
    heads = dt_raw.shape[1]
    channels = float(width * lax.axis_size(("y", "core")))
    steps = dt_raw.T
    a_log, dt_bias = a_log[None, :], dt_bias[None, :]
    skip_d, gain = skip_d[None, :], norm_gain[None, :]
    message = like((GROUP, STATE + 8, LANES))
    wide = like((rows, width))
    small = like((rows, heads))
    turned = like((heads, rows))

    own, summed, deltas = call(
        states_kernel,
        [message, small, small],
        lengths,
        inputs_x,
        input_b,
        steps,
        a_log,
        dt_bias,
        hbm=True,
        scratch=[
            pltpu.SMEM(lengths.shape, jnp.int32),
            pltpu.VMEM(inputs_x.shape, BF16),
            pltpu.VMEM(input_b.shape, BF16),
            pltpu.VMEM(steps.shape, F32),
            pltpu.VMEM(a_log.shape, F32),
            pltpu.VMEM(dt_bias.shape, F32),
            pltpu.SemaphoreType.DMA((6,)),
        ],
    )

    def before():
        return call(
            within_kernel,
            [wide, wide, wide, wide],
            lengths,
            inputs_x,
            gate_z,
            cotangent,
            input_b,
            input_c,
            summed,
            deltas,
            skip_d,
            smem=True,
        )

    entering, marks, (within, fresh, gate, gated) = carry(own, before)
    core, bent, sums = call(
        output_kernel,
        [wide, wide, like((1, 2 * rows // LANES, LANES))],
        within,
        fresh,
        gate,
        gated,
        input_c,
        gain,
        entering,
    )
    sums = lax.all_gather(sums[0], "core").sum(0)
    sums = exchange(jnp.broadcast_to(sums, (lax.axis_size("y"),) + sums.shape), "y")
    pulled, own_back = call(
        functools.partial(pull_kernel, channels),
        [wide, message],
        core,
        bent,
        gated,
        fresh,
        input_c,
        gain,
        sums,
    )

    def after():
        return call(
            inner_kernel,
            [
                wide,
                wide,
                like((rows, width), BF16),
                like((rows, width), BF16),
                like((STATE, width)),
                like((rows, STATE)),
                like((rows, STATE), BF16),
                turned,
                turned,
            ],
            lengths,
            inputs_x,
            input_b,
            input_c,
            summed,
            deltas,
            skip_d,
            core,
            pulled,
            fresh,
            entering,
            own,
            smem=True,
        )

    later, gains, beside = carry_back(own_back, marks, after)
    base, weights, high, low, leaving, b_part, grad_c, along, back = beside
    share = width // (GROUP * lax.axis_size("zh"))
    grad_x, grad_b, grad_dt, grad_gain = call(
        final_kernel,
        [like((rows, width), BF16), like((rows, STATE), BF16), turned, like((1, share))],
        inputs_x,
        input_b,
        steps,
        a_log,
        dt_bias,
        base,
        weights,
        high,
        low,
        leaving,
        b_part,
        along,
        back,
        later,
        gains,
    )
    return (grad_x, grad_b, grad_c, grad_dt.T, grad_gain[0])


def solution(mesh):
    count, across = mesh.devices.shape
    split_mesh = Mesh(
        mesh.devices.reshape(count // GROUP, 2, GROUP // 2, across // 2, 2),
        ("zh", "zl", "x", "y", "core"),
    )
    tokens = ("zh", "zl", "x")
    heads = ("y", "core")
    both = P(tokens, heads)
    alone = P(heads)
    return jax.shard_map(
        per_device,
        mesh=split_mesh,
        in_specs=(both, both, both, both, both, alone, alone, alone, alone, P(), both),
        out_specs=(both, both, both, both, P(heads + tokens)),
        check_vma=False,
    )
```
